512 devices in a mesh: ctx: 64 (over y, z_lo, core), head: 8 (over x, z_hi).
Axes of the slice: x: 4, y: 8, z: 8 (z_hi: 2, z_lo: 4; z = z_hi * 4 + z_lo), core: 2. Of those that a mesh axis runs over, the one named last changes fastest.
Arguments:
- queries: bfloat16 [32768, 8192], P(('ctx', 'head')), may hold values from -72 to 72
- keys: bfloat16 [32768, 1024], P(('ctx', 'head')), may hold values from -4 to 4
- values: bfloat16 [32768, 1024], P(('ctx', 'head')), may hold values from -6 to 6
- assignment: int32 [64], replicated, may hold values from 0 to 63, each once
- anchor: int32 [1], replicated, may hold values from 0 to 63
- lengths: int32 [64], replicated, may hold values from 257 to 512
Outputs:
- attended: bfloat16 [32768, 8192], P(('ctx', 'head'))
The draws below stay inside these ranges and needn't reach their ends.
Inputs may be any that keep to these rules, and one draw needn't show every extreme that they name: `assignment`: every block number appears once.
All inputs are finite; a program needn't handle non-finite values.
Results may differ from the reference program's by a relative error of at most 0.0027.
Values may be sent and summed in bfloat16 or wider, within the bound.
No kernel may reach another device: no remote copies, remote signals or barrier semaphores. Data moves between devices by JAX's collectives and lax.ppermute only.
A program may use at most 64 MiB of HBM per device.

```python
import math
import jax
import jax.numpy as jnp
from jax import lax

HEADS = 64
KV_HEADS = 8
HEAD_DIM = 128
BLOCK = 512
BLOCKS = 64
TOKENS = 32768


def draw_keys(key, part):
    key = jax.random.fold_in(key, 11)
    drawn = jnp.clip(jax.random.normal(key, (TOKENS, KV_HEADS, HEAD_DIM), jnp.float32), -4.0, 4.0)
    return drawn.reshape(TOKENS, KV_HEADS * HEAD_DIM).astype(jnp.bfloat16)


def draw_queries(key, part):
    key = jax.random.fold_in(key, 12)
    drawn = jnp.clip(2.5 * jax.random.normal(key, (TOKENS, HEADS, HEAD_DIM), jnp.float32), -15.0, 15.0)
    return drawn.reshape(TOKENS, HEADS * HEAD_DIM).astype(jnp.bfloat16)


def draw_lengths(key, part):
    key = jax.random.fold_in(key, 13)
    first_key, second_key = jax.random.split(key)
    drawn = BLOCK - jax.random.randint(first_key, (BLOCKS,), 0, BLOCK // 2)
    spot = jax.random.randint(second_key, (), 0, BLOCKS)
    return jnp.where(jnp.arange(BLOCKS) == spot, BLOCK, drawn).astype(jnp.int32)


def levels(stream_key, dims, shards, low, largest):
    level = 1.0
    for axis_at, shards_of in shards:
        draws = jax.random.uniform(jax.random.fold_in(jax.random.fold_in(stream_key, 6), axis_at), (shards_of,), jnp.float32, low / len(shards), largest / len(shards))
        level = level * jnp.repeat(jnp.exp(draws), dims[axis_at] // shards_of).reshape((-1,) + (1,) * (len(dims) - 1 - axis_at))
    return level


def gaussian(rng, extent, spread, most, cuts=(), held_as=jnp.bfloat16):
    values = jax.random.normal(rng, extent, jnp.float32) * spread
    if len(cuts) > 0:
        values = levels(rng, extent, cuts, -0.22, 0.18) * values
    return jnp.clip(values, min=-most, max=most).astype(held_as)


def setup_inputs(seed: int = 0) -> dict:
    key_list = jax.random.split(jax.random.key(seed), 7)
    return {
        "queries": draw_queries(jax.random.fold_in(key_list[6], 71), 0),
        "keys": draw_keys(jax.random.fold_in(key_list[6], 71), 0),
        "values": gaussian(key_list[2], (TOKENS, KV_HEADS * HEAD_DIM), 1.0, 6.0, ((0, 512),)),
        "assignment": jax.random.permutation(key_list[3], BLOCKS).astype(jnp.int32),
        "anchor": jax.random.randint(key_list[4], (1,), 0, BLOCKS).astype(jnp.int32),
        "lengths": draw_lengths(jax.random.fold_in(key_list[6], 71), 0),
    }


def attend_tile(query_tile, query_pos, own_keys, own_vals, anc_keys, anc_vals, my_len, anc_len, is_anchor):
    factor = 1.0 / math.sqrt(query_tile.shape[-1])
    key_pos = jnp.arange(own_keys.shape[0], dtype=jnp.int32)

    def attend_part(key_set, val_set, keep):
        scores = jnp.dot(query_tile, key_set.T, preferred_element_type=jnp.float32) * factor
        scores = jnp.where(keep, scores, -jnp.inf)
        row_max = lax.optimization_barrier(jnp.max(scores, axis=1, keepdims=True))
        weights = jnp.exp(scores - row_max)
        row_sum = lax.optimization_barrier(jnp.sum(weights, axis=1, keepdims=True))
        result = jnp.dot(weights.astype(jnp.bfloat16), val_set, preferred_element_type=jnp.float32) / row_sum
        return (result, row_max + jnp.log(row_sum))
    own_mask = (key_pos[None, :] <= query_pos[:, None]) & (key_pos[None, :] < my_len)
    anc_mask = jnp.broadcast_to(key_pos[None, :] < anc_len, own_mask.shape)
    own_out, own_lse = attend_part(own_keys, own_vals, own_mask)
    anc_out, anc_lse = attend_part(anc_keys, anc_vals, anc_mask)
    anc_lse = jnp.where(is_anchor, -jnp.inf, anc_lse)
    biggest = jnp.maximum(own_lse, anc_lse)
    own_weight = jnp.exp(own_lse - biggest)
    anc_weight = jnp.where(is_anchor, jnp.zeros_like(own_weight), jnp.exp(anc_lse - biggest))
    merged = (own_weight * own_out + anc_weight * anc_out) / (own_weight + anc_weight)
    return merged.astype(jnp.bfloat16)

def reference(queries, keys, values, assignment, anchor, lengths):
    block_count = assignment.shape[0]
    block_len = queries.shape[0] // block_count
    head_count = queries.shape[1] // HEAD_DIM
    kv_heads = keys.shape[1] // HEAD_DIM
    per_group = head_count // kv_heads
    query_all = queries.reshape(block_count, block_len, head_count, HEAD_DIM)
    keys_all = keys.reshape(block_count, block_len, kv_heads, HEAD_DIM)
    vals_all = values.reshape(block_count, block_len, kv_heads, HEAD_DIM)
    shard_ids = jnp.arange(block_count, dtype=jnp.int32)
    anchor_shard = jnp.sum(jnp.where(assignment == anchor[0], shard_ids, 0)).astype(jnp.int32)
    anc_keys = keys_all[anchor_shard]
    anc_vals = vals_all[anchor_shard]
    anc_len = lengths[anchor[0]]
    query_pos = jnp.arange(block_len, dtype=jnp.int32)

    def one_block(shard):
        block_id = assignment[shard]
        my_len = lengths[block_id]
        is_anchor = block_id == anchor[0]
        block_q = query_all[shard]
        block_k = keys_all[shard]
        block_v = vals_all[shard]

        def one_head(head_index):
            kv_index = head_index // per_group
            return attend_tile(block_q[:, head_index], query_pos, block_k[:, kv_index], block_v[:, kv_index], anc_keys[:, kv_index], anc_vals[:, kv_index], my_len, anc_len, is_anchor)
        per_head = lax.map(one_head, jnp.arange(head_count, dtype=jnp.int32))
        return jnp.transpose(per_head, (1, 0, 2)).reshape(block_len, head_count * HEAD_DIM)
    result = lax.map(one_block, shard_ids)
    return result.reshape(block_count * block_len, head_count * HEAD_DIM)
```

```python
import math

import jax
import jax.numpy as jnp
from jax import lax
from jax.experimental import pallas as pl
from jax.experimental.pallas import tpu as pltpu
from jax.sharding import Mesh, PartitionSpec as P

HEAD_DIM = 128
GROUP = 8
AXES = ("y", "zl", "core", "x", "zh")
SIZES = (8, 4, 2, 4, 2)
CHUNK = 4
SCALE = math.log2(math.e) / math.sqrt(HEAD_DIM)
NEG = -math.inf


def head_columns(g, c):
    first = g * GROUP + c * CHUNK
    return [
        pl.ds(pl.multiple_of((first + i) * HEAD_DIM, HEAD_DIM), HEAD_DIM) for i in range(CHUNK)
    ]


def attend_set(q_ref, cols, k, v, bias):
    rows = q_ref.shape[0]
    q = jnp.concatenate([q_ref[:, at] for at in cols], axis=0)
    s = lax.dot_general(q, k, (((1,), (1,)), ((), ())), preferred_element_type=jnp.float32)
    s = (s.reshape(CHUNK, rows, -1) + bias[None]).reshape(CHUNK * rows, -1)
    m = jnp.max(s, axis=1, keepdims=True)
    e = jnp.exp2((s - m) * SCALE)
    l = jnp.sum(e, axis=1, keepdims=True)
    return m, l, jnp.dot(e.astype(jnp.bfloat16), v, preferred_element_type=jnp.float32)


def own_kernel(meta, q_ref, kv_ref, o_ref, stat_ref, bias_ref):
    rows = q_ref.shape[0]
    head_me, my_len = meta[0], meta[1]
    col = lax.broadcasted_iota(jnp.int32, bias_ref.shape, 1)
    row = lax.broadcasted_iota(jnp.int32, bias_ref.shape, 0) + head_me * rows
    bias_ref[...] = jnp.where((col <= row) & (col < my_len), 0.0, NEG)
    first = lax.broadcasted_iota(jnp.int32, (CHUNK * rows, HEAD_DIM), 1) == 0

    def one_group(g, carry):
        k = kv_ref[:, pl.ds(pl.multiple_of(g * HEAD_DIM, HEAD_DIM), HEAD_DIM)]
        v = kv_ref[:, pl.ds(pl.multiple_of((8 + g) * HEAD_DIM, HEAD_DIM), HEAD_DIM)]
        for c in range(GROUP // CHUNK):
            m, l, o = attend_set(q_ref, head_columns(g, c), k, v, bias_ref[...])
            at = pl.ds(c * CHUNK * rows, CHUNK * rows)
            o_ref[g, at] = o
            stat_ref[g, at] = jnp.where(first, m, l)
        return carry

    lax.fori_loop(0, 8, one_group, 0)


def anchor_kernel(meta, q_ref, mine_ref, other_ref, o_ref, stat_ref, out_ref, bias_ref):
    rows = q_ref.shape[0]
    anc_len, is_anchor, core = meta[2], meta[3], meta[4]
    col = lax.broadcasted_iota(jnp.int32, bias_ref.shape, 1)
    bias_ref[...] = jnp.where(col < anc_len, 0.0, NEG)

    def one_group(g, carry):
        mine = mine_ref[:, g].reshape(512, HEAD_DIM)
        other = other_ref[:, g].reshape(512, HEAD_DIM)
        k = jnp.where(core == 0, mine, other)
        v = jnp.where(core == 0, other, mine)
        for c in range(GROUP // CHUNK):
            cols = head_columns(g, c)
            m1, l1, o1 = attend_set(q_ref, cols, k, v, bias_ref[0:1, :])
            m1 = jnp.where(is_anchor > 0, NEG, m1)
            at = pl.ds(c * CHUNK * rows, CHUNK * rows)
            m0, l0 = stat_ref[g, at, 0:1], stat_ref[g, at, 1:2]
            big = jnp.maximum(m0, m1)
            w0 = jnp.exp2((m0 - big) * SCALE)
            w1 = jnp.exp2((m1 - big) * SCALE)
            inv = 1.0 / (w0 * l0 + w1 * l1)
            o = ((w0 * inv) * o_ref[g, at] + (w1 * inv) * o1).astype(out_ref.dtype)
            for i, to in enumerate(cols):
                out_ref[:, to] = o[i * rows : (i + 1) * rows]
        return carry

    lax.fori_loop(0, 8, one_group, 0)


VMEM = pl.BlockSpec(memory_space=pltpu.VMEM)
SMEM = pl.BlockSpec(memory_space=pltpu.SMEM)
COST = pl.CostEstimate(flops=2**30, bytes_accessed=6 * 2**20, transcendentals=2**21)
PARAMS = pltpu.CompilerParams(vmem_limit_bytes=40 * 1024 * 1024)


def attend_own(meta, queries, own, interpret=False):
    rows = queries.shape[0]
    part = jax.ShapeDtypeStruct((8, GROUP * rows, HEAD_DIM), jnp.float32)
    return pl.pallas_call(
        own_kernel,
        out_shape=(part, part),
        in_specs=[SMEM, VMEM, VMEM],
        out_specs=(VMEM, VMEM),
        scratch_shapes=[pltpu.VMEM((rows, 512), jnp.float32)],
        compiler_params=PARAMS,
        cost_estimate=COST,
        interpret=interpret,
    )(meta, queries, own)


def attend_anchor(meta, queries, mine, other, o, stat, interpret=False):
    return pl.pallas_call(
        anchor_kernel,
        out_shape=jax.ShapeDtypeStruct(queries.shape, jnp.bfloat16),
        in_specs=[SMEM] + [VMEM] * 5,
        out_specs=VMEM,
        scratch_shapes=[pltpu.VMEM((8, 512), jnp.float32)],
        compiler_params=PARAMS,
        cost_estimate=COST,
        interpret=interpret,
    )(meta, queries, mine, other, o, stat)


def attend(meta, queries, own, anc, interpret=False):
    o, stat = attend_own(meta, queries, own, interpret)
    return attend_anchor(meta, queries, *anc, o, stat, interpret)


def swap(a, axis):
    return lax.ppermute(a, axis, [(0, 1), (1, 0)])


def exchange(a, axes):
    return lax.all_to_all(a, axes, split_axis=0, concat_axis=0, tiled=True)


def to_all(a, axes, n):
    return exchange(jnp.broadcast_to(a[None], (n,) + a.shape), axes)


def communicate(keys, values, anchor_shard):
    rows = keys.shape[0]
    zh = lax.axis_index("zh")
    kv = jnp.concatenate([keys, values], axis=1)
    other = swap(kv, "zh")
    pair = jnp.where(zh == 0, jnp.stack([kv, other]), jnp.stack([other, kv]))
    own = to_all(pair, "x", 4).reshape(8 * rows, -1)
    cut = [a.reshape(rows, 8, HEAD_DIM).transpose(1, 0, 2) for a in (keys, values)]
    got = exchange(jnp.stack(cut, axis=1).reshape(16, rows, HEAD_DIM), ("y", "core"))
    source = (anchor_shard >> 3) * 2 + (anchor_shard & 1)
    part = lax.dynamic_index_in_dim(got, source, 0, keepdims=False)
    part = to_all(part, ("zl", "zh"), 8).reshape(4, 2, rows, HEAD_DIM)
    part = lax.dynamic_index_in_dim(part, (anchor_shard >> 1) & 3, 0, keepdims=False)
    part = to_all(part, "y", 8)
    mine = to_all(part, "x", 4)
    return own, (mine, swap(mine, "core"))


def shards(queries, keys, values, assignment, anchor, lengths):
    ids = jnp.arange(assignment.shape[0], dtype=jnp.int32)
    y, zl, core, x, zh = (lax.axis_index(a) for a in AXES)
    my_index = (y * 4 + zl) * 2 + core
    block_id = jnp.sum(jnp.where(ids == my_index, assignment, 0))
    anchor_shard = jnp.sum(jnp.where(assignment == anchor[0], ids, 0))
    my_len = jnp.sum(jnp.where(ids == block_id, lengths, 0))
    anc_len = jnp.sum(jnp.where(ids == anchor[0], lengths, 0))
    is_anchor = (block_id == anchor[0]).astype(jnp.int32)
    meta = jnp.stack([x * 2 + zh, my_len, anc_len, is_anchor, core]).astype(jnp.int32)
    own, anc = communicate(keys, values, anchor_shard)
    return attend(meta, queries, own, anc)


def solution(mesh):
    fine = Mesh(mesh.devices.reshape(SIZES), AXES)
    spec = P(AXES, None)
    return jax.shard_map(
        shards,
        mesh=fine,
        in_specs=(spec, spec, spec, P(), P(), P()),
        out_specs=spec,
        check_vma=False,
    )
```

```python
import math

import jax
import jax.numpy as jnp
from jax import lax
from jax.experimental import pallas as pl
from jax.experimental.pallas import tpu as pltpu
from jax.sharding import Mesh, PartitionSpec as P

HEAD_DIM = 128
GROUP = 8
KV_HEADS = 8
WIDTH = GROUP * HEAD_DIM
AXES = ("y", "zl", "core", "x", "zh")
SIZES = (8, 4, 2, 4, 2)
CHUNK = 4
SCALE = math.log2(math.e) / math.sqrt(HEAD_DIM)
NEG = -math.inf


def group_columns(g):
    return pl.ds(pl.multiple_of(g * WIDTH, WIDTH), WIDTH)


def attend_set(q_ref, c, k, v, bias):
    rows = q_ref.shape[0]
    first = c * CHUNK * HEAD_DIM
    q = jnp.concatenate(
        [q_ref[:, first + i * HEAD_DIM : first + (i + 1) * HEAD_DIM] for i in range(CHUNK)], axis=0
    )
    s = lax.dot_general(q, k, (((1,), (1,)), ((), ())), preferred_element_type=jnp.float32)
    s = (s.reshape(CHUNK, rows, -1) + bias[None]).reshape(CHUNK * rows, -1)
    m = jnp.max(s, axis=1, keepdims=True)
    e = jnp.exp2((s - m) * SCALE)
    l = jnp.sum(e, axis=1, keepdims=True)
    o = jnp.dot(e.astype(jnp.bfloat16), v, preferred_element_type=jnp.float32)
    return m, l, o


def query_copy(q_hbm, q_buf, sem, g):
    return pltpu.make_async_copy(q_hbm.at[:, group_columns(g)], q_buf.at[g], sem.at[g])


def own_kernel(me, assignment, lengths, q_hbm, *refs):
    pair_refs, (o_ref, lse_ref, bias_ref, q_buf, sem) = refs[:4], refs[4:]
    rows = q_buf.shape[1]
    for g in range(KV_HEADS):
        query_copy(q_hbm, q_buf, sem, g).start()
    head_me = me[0] & 7
    my_len = lengths[assignment[me[0] >> 3]]
    col = lax.broadcasted_iota(jnp.int32, bias_ref.shape, 1)
    row = lax.broadcasted_iota(jnp.int32, bias_ref.shape, 0) + head_me * rows
    pos = (((head_me >> 1) - (col >> 7)) & 3) * 2 * rows + (col & 127)
    bias_ref[...] = jnp.where((pos <= row) & (pos < my_len), 0.0, NEG)

    def column(at):
        cols = pl.ds(pl.multiple_of(at * HEAD_DIM, HEAD_DIM), HEAD_DIM)
        return jnp.concatenate([r[:, :, cols].reshape(2 * rows, HEAD_DIM) for r in pair_refs], axis=0)

    def one_group(g, carry):
        k = column(g)
        v = column(KV_HEADS + g)
        query_copy(q_hbm, q_buf, sem, g).wait()
        for c in range(GROUP // CHUNK):
            m, l, o = attend_set(q_buf.at[g], c, k, v, bias_ref[...])
            at = pl.ds(c * CHUNK * rows, CHUNK * rows)
            o_ref[g, at] = o * (1.0 / l)
            lse_ref[g, at] = jnp.broadcast_to(m * SCALE + jnp.log2(l), o.shape)
        return carry

    lax.fori_loop(0, KV_HEADS, one_group, 0)


def out_copy(out_buf, out_hbm, sem, g):
    return pltpu.make_async_copy(out_buf.at[g], out_hbm.at[:, group_columns(g)], sem.at[g])


def anchor_kernel(
    me, assignment, anchor, lengths, q_hbm, mine_ref, other_ref, o_ref, lse_ref, out_hbm,
    bias_ref, q_buf, out_buf, q_sem, out_sem
):
    rows = q_buf.shape[1]
    for g in range(KV_HEADS):
        query_copy(q_hbm, q_buf, q_sem, g).start()
    anc_len = lengths[anchor[0]]
    is_anchor = assignment[me[0] >> 3] == anchor[0]
    core = (me[0] >> 3) & 1
    col = lax.broadcasted_iota(jnp.int32, bias_ref.shape, 1)
    bias_ref[...] = jnp.where(col < anc_len, 0.0, NEG)

    def one_group(g, carry):
        mine = mine_ref[:, g].reshape(512, HEAD_DIM)
        other = other_ref[:, g].reshape(512, HEAD_DIM)
        k = jnp.where(core == 0, mine, other)
        v = jnp.where(core == 0, other, mine)
        query_copy(q_hbm, q_buf, q_sem, g).wait()
        for c in range(GROUP // CHUNK):
            m1, l1, o1 = attend_set(q_buf.at[g], c, k, v, bias_ref[0:1, :])
            at = pl.ds(c * CHUNK * rows, CHUNK * rows)
            lse1 = jnp.where(is_anchor, NEG, m1 * SCALE + jnp.log2(l1))
            share = 1.0 / (1.0 + jnp.exp2(lse_ref[g, at] - lse1))
            o = (1.0 - share) * o_ref[g, at] + (share * (1.0 / l1)) * o1
            o = o.astype(out_buf.dtype)
            for i in range(CHUNK):
                to = (c * CHUNK + i) * HEAD_DIM
                out_buf[g, :, to : to + HEAD_DIM] = o[i * rows : (i + 1) * rows]
        out_copy(out_buf, out_hbm, out_sem, g).start()
        return carry

    lax.fori_loop(0, KV_HEADS, one_group, 0)
    for g in range(KV_HEADS):
        out_copy(out_buf, out_hbm, out_sem, g).wait()


VMEM = pl.BlockSpec(memory_space=pltpu.VMEM)
SMEM = pl.BlockSpec(memory_space=pltpu.SMEM)
HBM = pl.BlockSpec(memory_space=pltpu.HBM)
COST = pl.CostEstimate(flops=2**30, bytes_accessed=6 * 2**20, transcendentals=2**21)
PARAMS = pltpu.CompilerParams(vmem_limit_bytes=20 * 1024 * 1024)


def attend_own(me, assignment, lengths, queries, own, interpret=False):
    rows = queries.shape[0]
    part = jax.ShapeDtypeStruct((KV_HEADS, GROUP * rows, HEAD_DIM), jnp.float32)
    return pl.pallas_call(
        own_kernel,
        out_shape=(part, part),
        in_specs=[SMEM, SMEM, SMEM, HBM] + [VMEM] * 4,
        out_specs=(VMEM, VMEM),
        scratch_shapes=[
            pltpu.VMEM((rows, 512), jnp.float32),
            pltpu.VMEM((KV_HEADS, rows, WIDTH), jnp.bfloat16),
            pltpu.SemaphoreType.DMA((KV_HEADS,)),
        ],
        compiler_params=PARAMS,
        cost_estimate=COST,
        interpret=interpret,
    )(me, assignment, lengths, queries, *own)


def attend_anchor(me, assignment, anchor, lengths, queries, mine, other, o, lse, interpret=False):
    rows = queries.shape[0]
    return pl.pallas_call(
        anchor_kernel,
        out_shape=jax.ShapeDtypeStruct(queries.shape, jnp.bfloat16),
        in_specs=[SMEM] * 4 + [HBM] + [VMEM] * 4,
        out_specs=HBM,
        scratch_shapes=[
            pltpu.VMEM((8, 512), jnp.float32),
            pltpu.VMEM((KV_HEADS, rows, WIDTH), jnp.bfloat16),
            pltpu.VMEM((KV_HEADS, rows, WIDTH), jnp.bfloat16),
            pltpu.SemaphoreType.DMA((KV_HEADS,)),
            pltpu.SemaphoreType.DMA((KV_HEADS,)),
        ],
        compiler_params=PARAMS,
        cost_estimate=COST,
        interpret=interpret,
    )(me, assignment, anchor, lengths, queries, mine, other, o, lse)


def cut_kernel(k_ref, v_ref, kv_ref, piece_ref):
    half = k_ref.shape[1]
    kv_ref[:, :half] = k_ref[...]
    kv_ref[:, half:] = v_ref[...]
    for core, ref in enumerate((k_ref, v_ref)):
        for g in range(KV_HEADS):
            block = ref[:, g * HEAD_DIM : (g + 1) * HEAD_DIM]
            piece_ref[g, core] = block


def cut(keys, values, interpret=False):
    rows, width = keys.shape
    return pl.pallas_call(
        cut_kernel,
        out_shape=(
            jax.ShapeDtypeStruct((rows, 2 * width), keys.dtype),
            jax.ShapeDtypeStruct((KV_HEADS, 2, rows, HEAD_DIM), keys.dtype),
        ),
        in_specs=[VMEM, VMEM],
        out_specs=(VMEM, VMEM),
        interpret=interpret,
    )(keys, values)


def to_all(a, axes, n):
    return exchange(jnp.broadcast_to(a[None], (n,) + a.shape), axes)


def swap(a, axis):
    return lax.ppermute(a, axis, [(0, 1), (1, 0)])


def exchange(a, axes):
    return lax.all_to_all(a, axes, split_axis=0, concat_axis=0, tiled=True)


def shift(a, axis, by):
    n = lax.axis_size(axis)
    return lax.ppermute(a, axis, [(i, (i + by) % n) for i in range(n)])


def run(me, zh, queries, keys, values, assignment, anchor, lengths, interpret=False):
    ids = jnp.arange(assignment.shape[0], dtype=jnp.int32)
    anchor_shard = jnp.sum(jnp.where(assignment == anchor[0], ids, 0))
    kv, pieces = cut(keys, values, interpret)
    got = exchange(pieces.reshape((16,) + pieces.shape[2:]), ("y", "core"))
    other = swap(kv, "zh")
    source = (anchor_shard >> 3) * 2 + (anchor_shard & 1)
    part = lax.dynamic_index_in_dim(got, source, 0, keepdims=False)
    part = to_all(part, ("zl", "zh"), 8)
    part = part.reshape((4, 2) + part.shape[1:])
    part = lax.dynamic_index_in_dim(part, (anchor_shard >> 1) & 3, 0, keepdims=False)
    part, other = lax.optimization_barrier((part, other))
    pair = jnp.where(zh == 0, jnp.stack([kv, other]), jnp.stack([other, kv]))
    own = [pair] + [shift(pair, "x", s) for s in range(1, 4)]
    part = to_all(part, "y", 8)
    mine = to_all(part, "x", 4)
    o, lse = attend_own(me, assignment, lengths, queries, own, interpret)
    mine, o, lse = lax.optimization_barrier((mine, o, lse))
    theirs = swap(mine, "core")
    return attend_anchor(
        me, assignment, anchor, lengths, queries, mine, theirs, o, lse, interpret
    )


def shards(queries, keys, values, assignment, anchor, lengths):
    me = lax.axis_index(AXES).astype(jnp.int32).reshape(1)
    zh = lax.axis_index("zh")
    return run(me, zh, queries, keys, values, assignment, anchor, lengths)


def solution(mesh):
    fine = Mesh(mesh.devices.reshape(SIZES), AXES)
    spec = P(AXES, None)
    return jax.shard_map(
        shards,
        mesh=fine,
        in_specs=(spec, spec, spec, P(), P(), P()),
        out_specs=spec,
        check_vma=False,
    )
```

```python
import math

import jax
import jax.numpy as jnp
from jax import lax
from jax.experimental import pallas as pl
from jax.experimental.pallas import tpu as pltpu
from jax.sharding import Mesh, PartitionSpec as P

HEAD_DIM = 128
GROUP = 8
KV_HEADS = 8
WIDTH = GROUP * HEAD_DIM
AXES = ("y", "zl", "core", "x", "zh")
SIZES = (8, 4, 2, 4, 2)
CHUNK = 4
SCALE = math.log2(math.e) / math.sqrt(HEAD_DIM)
NEG = -math.inf


def group_columns(g):
    return pl.ds(pl.multiple_of(g * WIDTH, WIDTH), WIDTH)


def attend_set(q_ref, c, k, v, bias):
    rows = q_ref.shape[0]
    first = c * CHUNK * HEAD_DIM
    q = jnp.concatenate(
        [q_ref[:, first + i * HEAD_DIM : first + (i + 1) * HEAD_DIM] for i in range(CHUNK)], axis=0
    )
    s = lax.dot_general(q, k, (((1,), (1,)), ((), ())), preferred_element_type=jnp.float32)
    s = (s.reshape(CHUNK, rows, -1) + bias[None]).reshape(CHUNK * rows, -1)
    m = jnp.max(s, axis=1, keepdims=True)
    e = jnp.exp2((s - m) * SCALE)
    l = jnp.sum(e, axis=1, keepdims=True)
    o = jnp.dot(e.astype(jnp.bfloat16), v, preferred_element_type=jnp.float32)
    return m, l, o


def query_copy(q_hbm, q_buf, sem, g):
    return pltpu.make_async_copy(q_hbm.at[:, group_columns(g)], q_buf.at[g], sem.at[g])


def own_kernel(me, assignment, lengths, q_hbm, *refs):
    pairs_hbm, (o_hbm, lse_hbm) = refs[:4], refs[4:6]
    bias_ref, q_buf, kv_buf, o_buf, lse_buf, q_sem, kv_sem, o_sem, lse_sem = refs[6:]
    rows = q_buf.shape[1]
    pair_copies = [
        pltpu.make_async_copy(ref, kv_buf.at[i], kv_sem.at[i]) for i, ref in enumerate(pairs_hbm)
    ]
    for copy in pair_copies:
        copy.start()
    for g in range(KV_HEADS):
        query_copy(q_hbm, q_buf, q_sem, g).start()
    head_me = me[0] & 7
    my_len = lengths[assignment[me[0] >> 3]]
    col = lax.broadcasted_iota(jnp.int32, bias_ref.shape, 1)
    row = lax.broadcasted_iota(jnp.int32, bias_ref.shape, 0) + head_me * rows
    pos = (((head_me >> 1) - (col >> 7)) & 3) * 2 * rows + (col & 127)
    bias_ref[...] = jnp.where((pos <= row) & (pos < my_len), 0.0, NEG)
    for copy in pair_copies:
        copy.wait()

    def column(at):
        cols = pl.ds(pl.multiple_of(at * HEAD_DIM, HEAD_DIM), HEAD_DIM)
        return kv_buf[:, :, :, cols].reshape(8 * rows, HEAD_DIM)

    def result_copies(g):
        return (
            pltpu.make_async_copy(o_buf.at[g], o_hbm.at[g], o_sem.at[g]),
            pltpu.make_async_copy(lse_buf.at[g], lse_hbm.at[g], lse_sem.at[g]),
        )

    def one_group(g, carry):
        k = column(g)
        v = column(KV_HEADS + g)
        query_copy(q_hbm, q_buf, q_sem, g).wait()
        for c in range(GROUP // CHUNK):
            m, l, o = attend_set(q_buf.at[g], c, k, v, bias_ref[...])
            at = pl.ds(c * CHUNK * rows, CHUNK * rows)
            o_buf[g, at] = o * (1.0 / l)
            lse_buf[g, at] = jnp.broadcast_to(m * SCALE + jnp.log2(l), o.shape)
        for copy in result_copies(g):
            copy.start()
        return carry

    lax.fori_loop(0, KV_HEADS, one_group, 0)
    for g in range(KV_HEADS):
        for copy in result_copies(g):
            copy.wait()


def anchor_kernel(
    me, assignment, anchor, lengths, q_hbm, mine_hbm, theirs_hbm, o_hbm, lse_hbm, out_hbm,
    bias_ref, q_buf, mine_buf, theirs_buf, o_buf, lse_buf, out_buf, q_sem, in_sem, out_sem
):
    rows = q_buf.shape[1]

    def group_copies(g):
        return (
            query_copy(q_hbm, q_buf, q_sem, g),
            pltpu.make_async_copy(mine_hbm.at[:, g], mine_buf.at[g], in_sem.at[0, g]),
            pltpu.make_async_copy(theirs_hbm.at[:, g], theirs_buf.at[g], in_sem.at[1, g]),
            pltpu.make_async_copy(o_hbm.at[g], o_buf.at[g], in_sem.at[2, g]),
            pltpu.make_async_copy(lse_hbm.at[g], lse_buf.at[g], in_sem.at[3, g]),
        )

    def out_copy(g):
        return pltpu.make_async_copy(out_buf.at[g], out_hbm.at[:, group_columns(g)], out_sem.at[g])

    for g in range(KV_HEADS):
        for copy in group_copies(g):
            copy.start()
    anc_len = lengths[anchor[0]]
    is_anchor = assignment[me[0] >> 3] == anchor[0]
    core = (me[0] >> 3) & 1
    col = lax.broadcasted_iota(jnp.int32, bias_ref.shape, 1)
    bias_ref[...] = jnp.where(col < anc_len, 0.0, NEG)

    def one_group(g, carry):
        for copy in group_copies(g):
            copy.wait()
        mine = mine_buf[g].reshape(8 * rows, HEAD_DIM)
        theirs = theirs_buf[g].reshape(8 * rows, HEAD_DIM)
        k = jnp.where(core == 0, mine, theirs)
        v = jnp.where(core == 0, theirs, mine)
        for c in range(GROUP // CHUNK):
            m1, l1, o1 = attend_set(q_buf.at[g], c, k, v, bias_ref[0:1, :])
            at = pl.ds(c * CHUNK * rows, CHUNK * rows)
            lse1 = jnp.where(is_anchor, NEG, m1 * SCALE + jnp.log2(l1))
            share = 1.0 / (1.0 + jnp.exp2(lse_buf[g, at] - lse1))
            o = (1.0 - share) * o_buf[g, at] + (share * (1.0 / l1)) * o1
            o = o.astype(out_buf.dtype)
            for i in range(CHUNK):
                to = (c * CHUNK + i) * HEAD_DIM
                out_buf[g, :, to : to + HEAD_DIM] = o[i * rows : (i + 1) * rows]
        out_copy(g).start()
        return carry

    lax.fori_loop(0, KV_HEADS, one_group, 0)
    for g in range(KV_HEADS):
        out_copy(g).wait()


VMEM = pl.BlockSpec(memory_space=pltpu.VMEM)
SMEM = pl.BlockSpec(memory_space=pltpu.SMEM)
ANY = pl.BlockSpec(memory_space=pl.ANY)
COST = pl.CostEstimate(flops=2**31, bytes_accessed=6 * 2**20, transcendentals=2**21)
LONG = pl.CostEstimate(flops=2**36, bytes_accessed=6 * 2**20, transcendentals=2**21)
PARAMS = pltpu.CompilerParams(vmem_limit_bytes=60 * 1024 * 1024)


def attend_own(me, assignment, lengths, queries, own, interpret=False):
    rows = queries.shape[0]
    part = jax.ShapeDtypeStruct((KV_HEADS, GROUP * rows, HEAD_DIM), jnp.float32)
    return pl.pallas_call(
        own_kernel,
        out_shape=(part, part),
        in_specs=[SMEM, SMEM, SMEM] + [ANY] * 5,
        out_specs=(ANY, ANY),
        scratch_shapes=[
            pltpu.VMEM((rows, 8 * rows), jnp.float32),
            pltpu.VMEM((KV_HEADS, rows, WIDTH), jnp.bfloat16),
            pltpu.VMEM((4,) + own[0].shape, jnp.bfloat16),
            pltpu.VMEM(part.shape, jnp.float32),
            pltpu.VMEM(part.shape, jnp.float32),
            pltpu.SemaphoreType.DMA((KV_HEADS,)),
            pltpu.SemaphoreType.DMA((4,)),
            pltpu.SemaphoreType.DMA((KV_HEADS,)),
            pltpu.SemaphoreType.DMA((KV_HEADS,)),
        ],
        compiler_params=PARAMS,
        cost_estimate=LONG,
        interpret=interpret,
    )(me, assignment, lengths, queries, *own)


def attend_anchor(me, assignment, anchor, lengths, queries, mine, theirs, o, lse, interpret=False):
    rows = queries.shape[0]
    group = (KV_HEADS, 4, 2, rows, HEAD_DIM)
    return pl.pallas_call(
        anchor_kernel,
        out_shape=jax.ShapeDtypeStruct(queries.shape, jnp.bfloat16),
        in_specs=[SMEM] * 4 + [ANY] * 5,
        out_specs=ANY,
        scratch_shapes=[
            pltpu.VMEM((8, 8 * rows), jnp.float32),
            pltpu.VMEM((KV_HEADS, rows, WIDTH), jnp.bfloat16),
            pltpu.VMEM(group, jnp.bfloat16),
            pltpu.VMEM(group, jnp.bfloat16),
            pltpu.VMEM(o.shape, jnp.float32),
            pltpu.VMEM(o.shape, jnp.float32),
            pltpu.VMEM((KV_HEADS, rows, WIDTH), jnp.bfloat16),
            pltpu.SemaphoreType.DMA((KV_HEADS,)),
            pltpu.SemaphoreType.DMA((4, KV_HEADS)),
            pltpu.SemaphoreType.DMA((KV_HEADS,)),
        ],
        compiler_params=PARAMS,
        cost_estimate=COST,
        interpret=interpret,
    )(me, assignment, anchor, lengths, queries, mine, theirs, o, lse)


def pair_kernel(me, kv_hbm, other_hbm, pair_hbm, sem):
    zh = me[0] & 1
    copies = (
        pltpu.make_async_copy(kv_hbm, pair_hbm.at[zh], sem.at[0]),
        pltpu.make_async_copy(other_hbm, pair_hbm.at[1 - zh], sem.at[1]),
    )
    for copy in copies:
        copy.start()
    for copy in copies:
        copy.wait()


def make_pair(me, kv, other, interpret=False):
    return pl.pallas_call(
        pair_kernel,
        out_shape=jax.ShapeDtypeStruct((2,) + kv.shape, kv.dtype),
        in_specs=[SMEM, ANY, ANY],
        out_specs=ANY,
        scratch_shapes=[pltpu.SemaphoreType.DMA((2,))],
        cost_estimate=LONG,
        interpret=interpret,
    )(me, kv, other)


def cut_kernel(k_ref, v_ref, kv_ref, piece_ref):
    half = k_ref.shape[1]
    kv_ref[:, :half] = k_ref[...]
    kv_ref[:, half:] = v_ref[...]
    for core, ref in enumerate((k_ref, v_ref)):
        for g in range(KV_HEADS):
            block = ref[:, g * HEAD_DIM : (g + 1) * HEAD_DIM]
            piece_ref[g, core] = block


def cut(keys, values, interpret=False):
    rows, width = keys.shape
    return pl.pallas_call(
        cut_kernel,
        out_shape=(
            jax.ShapeDtypeStruct((rows, 2 * width), keys.dtype),
            jax.ShapeDtypeStruct((KV_HEADS, 2, rows, HEAD_DIM), keys.dtype),
        ),
        in_specs=[VMEM, VMEM],
        out_specs=(VMEM, VMEM),
        interpret=interpret,
    )(keys, values)


def to_all(a, axes, n):
    return exchange(jnp.broadcast_to(a[None], (n,) + a.shape), axes)


def swap(a, axis):
    return lax.ppermute(a, axis, [(0, 1), (1, 0)])


def exchange(a, axes):
    return lax.all_to_all(a, axes, split_axis=0, concat_axis=0, tiled=True)


def shift(a, axis, by):
    n = lax.axis_size(axis)
    return lax.ppermute(a, axis, [(i, (i + by) % n) for i in range(n)])


def run(me, queries, keys, values, assignment, anchor, lengths, interpret=False):
    ids = jnp.arange(assignment.shape[0], dtype=jnp.int32)
    anchor_shard = jnp.sum(jnp.where(assignment == anchor[0], ids, 0))
    kv, pieces = cut(keys, values, interpret)
    got = exchange(pieces.reshape((16,) + pieces.shape[2:]), ("y", "core"))
    other = swap(kv, "zh")
    source = (anchor_shard >> 3) * 2 + (anchor_shard & 1)
    part = lax.dynamic_index_in_dim(got, source, 0, keepdims=False)
    part = to_all(part, ("zl", "zh"), 8)
    part = part.reshape((4, 2) + part.shape[1:])
    part = lax.dynamic_index_in_dim(part, (anchor_shard >> 1) & 3, 0, keepdims=False)
    pair = make_pair(me, kv, other, interpret)
    part, pair = lax.optimization_barrier((part, pair))
    own = [pair] + [shift(pair, "x", s) for s in range(1, 4)]
    part = to_all(part, "y", 8)
    mine = to_all(part, "x", 4)
    o, lse = attend_own(me, assignment, lengths, queries, own, interpret)
    mine, o, lse = lax.optimization_barrier((mine, o, lse))
    theirs = swap(mine, "core")
    return attend_anchor(
        me, assignment, anchor, lengths, queries, mine, theirs, o, lse, interpret
    )


def shards(queries, keys, values, assignment, anchor, lengths):
    me = lax.axis_index(AXES).astype(jnp.int32).reshape(1)
    return run(me, queries, keys, values, assignment, anchor, lengths)


def solution(mesh):
    fine = Mesh(mesh.devices.reshape(SIZES), AXES)
    spec = P(AXES, None)
    return jax.shard_map(
        shards,
        mesh=fine,
        in_specs=(spec, spec, spec, P(), P(), P()),
        out_specs=spec,
        check_vma=False,
    )
```

```python
import functools
import math

import jax
import jax.numpy as jnp
from jax import lax
from jax.experimental import pallas as pl
from jax.experimental.pallas import tpu as pltpu
from jax.sharding import Mesh, PartitionSpec as P

HEAD_DIM = 128
GROUP = 8
KV_HEADS = 8
HALF = 4
WIDTH = GROUP * HEAD_DIM
AXES = ("y", "zl", "core", "x", "zh")
SIZES = (8, 4, 2, 4, 2)
CHUNK = 4
SCALE = math.log2(math.e) / math.sqrt(HEAD_DIM)
NEG = -math.inf


def group_columns(g):
    return pl.ds(pl.multiple_of(g * WIDTH, WIDTH), WIDTH)


def attend_set(q_ref, c, k, v, bias):
    rows = q_ref.shape[0]
    first = c * CHUNK * HEAD_DIM
    q = jnp.concatenate(
        [q_ref[:, first + i * HEAD_DIM : first + (i + 1) * HEAD_DIM] for i in range(CHUNK)], axis=0
    )
    s = lax.dot_general(q, k, (((1,), (1,)), ((), ())), preferred_element_type=jnp.float32)
    free = s.shape[1] - bias.shape[1]
    tail = (s[:, free:].reshape(CHUNK, rows, -1) + bias[None]).reshape(CHUNK * rows, -1)
    s = jnp.concatenate([s[:, :free], tail], axis=1) if free else tail
    m = jnp.max(s, axis=1, keepdims=True)
    e = jnp.exp2((s - m) * SCALE)
    l = jnp.sum(e, axis=1, keepdims=True)
    o = jnp.dot(e.astype(jnp.bfloat16), v, preferred_element_type=jnp.float32)
    return m, l, o


def query_copy(q_hbm, q_buf, sem, g):
    return pltpu.make_async_copy(q_hbm.at[:, group_columns(g)], q_buf.at[g], sem.at[g])


def start_ahead(copies, g, count=KV_HEADS):
    def start():
        for copy in copies(g):
            copy.start()

    if isinstance(g, int):
        start()
    else:
        pl.when(g < count)(start)


def two_at_a_time(body, count):
    def step(i, carry):
        body(2 * i)
        body(2 * i + 1)
        return carry

    lax.fori_loop(0, count // 2, step, 0)


def own_kernel(me, assignment, lengths, q_hbm, *refs):
    pairs_hbm, (o_hbm, lse_hbm) = refs[:4], refs[4:6]
    bias_ref, q_buf, kv_buf, o_buf, lse_buf, q_sem, kv_sem, o_sem, lse_sem = refs[6:]
    rows = q_buf.shape[1]

    def group_copies(g):
        return [query_copy(q_hbm, q_buf, q_sem, g)] + [
            pltpu.make_async_copy(ref.at[:, g & 3, :, g >> 2], kv_buf.at[g, i], kv_sem.at[i, g])
            for i, ref in enumerate(pairs_hbm)
        ]

    start_ahead(group_copies, 0)
    start_ahead(group_copies, 1)
    head_me = me[0] & 7
    my_len = lengths[assignment[me[0] >> 3]]
    col = lax.broadcasted_iota(jnp.int32, bias_ref.shape, 1)
    row = lax.broadcasted_iota(jnp.int32, bias_ref.shape, 0) + head_me * rows
    pos = (((head_me >> 1) - (col >> 7)) & 3) * 2 * rows + (col & 127)
    bias_ref[...] = jnp.where((pos <= row) & (pos < my_len), 0.0, NEG)
    def result_copies(g):
        return (
            pltpu.make_async_copy(o_buf.at[g], o_hbm.at[g], o_sem.at[g]),
            pltpu.make_async_copy(lse_buf.at[g], lse_hbm.at[g], lse_sem.at[g]),
        )

    def one_group(g):
        start_ahead(group_copies, g + 2)
        for copy in group_copies(g):
            copy.wait()
        k = kv_buf[g, :, :, 0].reshape(8 * rows, HEAD_DIM)
        v = kv_buf[g, :, :, 1].reshape(8 * rows, HEAD_DIM)
        for c in range(GROUP // CHUNK):
            m, l, o = attend_set(q_buf.at[g], c, k, v, bias_ref[...])
            at = pl.ds(c * CHUNK * rows, CHUNK * rows)
            o_buf[g, at] = o * (1.0 / l)
            lse_buf[g, at] = jnp.broadcast_to(m * SCALE + jnp.log2(l), o.shape)
        for copy in result_copies(g):
            copy.start()

    two_at_a_time(one_group, KV_HEADS)
    for g in range(KV_HEADS):
        for copy in result_copies(g):
            copy.wait()


def anchor_kernel(which, me, assignment, anchor, lengths, q_hbm, kv_hbm, o_hbm, lse_hbm, *refs):
    out_hbm, bias_ref, q_buf, kv_buf, o_buf, lse_buf, out_buf, in_sem, out_sem = refs[-9:]
    rows = q_buf.shape[1]
    core = (me[0] >> 3) & 1
    first = (core ^ which) * HALF

    def group_copies(i):
        g = first + i
        return (
            pltpu.make_async_copy(q_hbm.at[:, group_columns(g)], q_buf.at[i], in_sem.at[0, i]),
            pltpu.make_async_copy(kv_hbm.at[:, pl.ds(2 * i, 2)], kv_buf.at[i], in_sem.at[1, i]),
            pltpu.make_async_copy(o_hbm.at[g], o_buf.at[i], in_sem.at[2, i]),
            pltpu.make_async_copy(lse_hbm.at[g], lse_buf.at[i], in_sem.at[3, i]),
        )

    def out_copy(i):
        to = out_hbm.at[:, group_columns(first + i)]
        return pltpu.make_async_copy(out_buf.at[i], to, out_sem.at[i])

    start_ahead(group_copies, 0)
    start_ahead(group_copies, 1)
    anc_len = lengths[anchor[0]]
    is_anchor = assignment[me[0] >> 3] == anchor[0]
    col = lax.broadcasted_iota(jnp.int32, bias_ref.shape, 1) + 256
    bias_ref[...] = jnp.where(col < anc_len, 0.0, NEG)

    def one_group(i):
        start_ahead(group_copies, i + 2, HALF)
        for copy in group_copies(i):
            copy.wait()
        k = kv_buf[i, :, 0].reshape(8 * rows, HEAD_DIM)
        v = kv_buf[i, :, 1].reshape(8 * rows, HEAD_DIM)
        for c in range(GROUP // CHUNK):
            m1, l1, o1 = attend_set(q_buf.at[i], c, k, v, bias_ref[0:1, :])
            at = pl.ds(c * CHUNK * rows, CHUNK * rows)
            lse1 = jnp.where(is_anchor, NEG, m1 * SCALE + jnp.log2(l1))
            share = 1.0 / (1.0 + jnp.exp2(lse_buf[i, at] - lse1))
            o = (1.0 - share) * o_buf[i, at] + (share * (1.0 / l1)) * o1
            o = o.astype(out_buf.dtype)
            for j in range(CHUNK):
                to = (c * CHUNK + j) * HEAD_DIM
                out_buf[i, :, to : to + HEAD_DIM] = o[j * rows : (j + 1) * rows]
        out_copy(i).start()

    two_at_a_time(one_group, HALF)
    for i in range(HALF):
        out_copy(i).wait()


VMEM = pl.BlockSpec(memory_space=pltpu.VMEM)
SMEM = pl.BlockSpec(memory_space=pltpu.SMEM)
ANY = pl.BlockSpec(memory_space=pl.ANY)
COST = pl.CostEstimate(flops=2**31, bytes_accessed=6 * 2**20, transcendentals=2**21)
LONG = pl.CostEstimate(flops=2**36, bytes_accessed=6 * 2**20, transcendentals=2**21)
PARAMS = pltpu.CompilerParams(vmem_limit_bytes=60 * 1024 * 1024)


def attend_own(me, assignment, lengths, queries, own, interpret=False):
    rows = queries.shape[0]
    part = jax.ShapeDtypeStruct((KV_HEADS, GROUP * rows, HEAD_DIM), jnp.float32)
    return pl.pallas_call(
        own_kernel,
        out_shape=(part, part),
        in_specs=[SMEM, SMEM, SMEM] + [ANY] * 5,
        out_specs=(ANY, ANY),
        scratch_shapes=[
            pltpu.VMEM((rows, 8 * rows), jnp.float32),
            pltpu.VMEM((KV_HEADS, rows, WIDTH), jnp.bfloat16),
            pltpu.VMEM((KV_HEADS, 4, 2, 2, rows, HEAD_DIM), jnp.bfloat16),
            pltpu.VMEM(part.shape, jnp.float32),
            pltpu.VMEM(part.shape, jnp.float32),
            pltpu.SemaphoreType.DMA((KV_HEADS,)),
            pltpu.SemaphoreType.DMA((4, KV_HEADS)),
            pltpu.SemaphoreType.DMA((KV_HEADS,)),
            pltpu.SemaphoreType.DMA((KV_HEADS,)),
        ],
        compiler_params=PARAMS,
        cost_estimate=LONG,
        interpret=interpret,
    )(me, assignment, lengths, queries, *own)


def attend_anchor(
    which, me, assignment, anchor, lengths, queries, kv, o, lse, out=None, interpret=False
):
    rows = queries.shape[0]
    extra = () if out is None else (out,)
    return pl.pallas_call(
        functools.partial(anchor_kernel, which),
        out_shape=jax.ShapeDtypeStruct(queries.shape, jnp.bfloat16),
        in_specs=[SMEM] * 4 + [ANY] * (4 + len(extra)),
        out_specs=ANY,
        input_output_aliases={8: 0} if extra else {},
        scratch_shapes=[
            pltpu.VMEM((8, 8 * rows - 256), jnp.float32),
            pltpu.VMEM((HALF, rows, WIDTH), jnp.bfloat16),
            pltpu.VMEM((HALF, 4, 2, 2, rows, HEAD_DIM), jnp.bfloat16),
            pltpu.VMEM((HALF,) + o.shape[1:], jnp.float32),
            pltpu.VMEM((HALF,) + o.shape[1:], jnp.float32),
            pltpu.VMEM((HALF, rows, WIDTH), jnp.bfloat16),
            pltpu.SemaphoreType.DMA((4, HALF)),
            pltpu.SemaphoreType.DMA((HALF,)),
        ],
        compiler_params=PARAMS,
        cost_estimate=COST,
        interpret=interpret,
    )(me, assignment, anchor, lengths, queries, kv, o, lse, *extra)


def pair_kernel(me, mine_ref, other_ref, pair_ref):
    zh = me[0] & 1
    pair_ref[zh] = mine_ref[...]
    pair_ref[1 - zh] = other_ref[...]


def make_pair(me, mine, other, interpret=False):
    return pl.pallas_call(
        pair_kernel,
        out_shape=jax.ShapeDtypeStruct((2,) + mine.shape, mine.dtype),
        in_specs=[SMEM, VMEM, VMEM],
        out_specs=VMEM,
        cost_estimate=LONG,
        interpret=interpret,
    )(me, mine, other)


def cut_kernel(k_ref, v_ref, piece_ref):
    for kind, ref in enumerate((k_ref, v_ref)):
        for g in range(KV_HEADS):
            piece_ref[g % HALF, kind, g // HALF] = ref[:, g * HEAD_DIM : (g + 1) * HEAD_DIM]


def cut(keys, values, interpret=False):
    return pl.pallas_call(
        cut_kernel,
        out_shape=jax.ShapeDtypeStruct((HALF, 2, 2, keys.shape[0], HEAD_DIM), keys.dtype),
        in_specs=[VMEM, VMEM],
        out_specs=VMEM,
        interpret=interpret,
    )(keys, values)


def to_all(a, axes, n):
    return exchange(jnp.broadcast_to(a[None], (n,) + a.shape), axes)


def swap(a, axis):
    return lax.ppermute(a, axis, [(0, 1), (1, 0)])


def exchange(a, axes):
    return lax.all_to_all(a, axes, split_axis=0, concat_axis=0, tiled=True)


def shift(a, axis, by):
    n = lax.axis_size(axis)
    return lax.ppermute(a, axis, [(i, (i + by) % n) for i in range(n)])


def run(me, queries, keys, values, assignment, anchor, lengths, interpret=False):
    ids = jnp.arange(assignment.shape[0], dtype=jnp.int32)
    anchor_shard = jnp.sum(jnp.where(assignment == anchor[0], ids, 0))
    pieces = cut(keys, values, interpret)
    got = exchange(pieces.reshape((16,) + pieces.shape[3:]), ("y", "core"))
    other = swap(pieces, "zh")
    source = (anchor_shard >> 3) * 2 + (anchor_shard & 1)
    part = lax.dynamic_index_in_dim(got, source, 0, keepdims=False)
    part = to_all(part, ("zl", "zh"), 8)
    part = part.reshape((4, 2) + part.shape[1:])
    part = lax.dynamic_index_in_dim(part, (anchor_shard >> 1) & 3, 0, keepdims=False)
    pair = make_pair(me, pieces, other, interpret)
    part, pair = lax.optimization_barrier((part, pair))
    own = [pair] + [shift(pair, "x", s) for s in range(1, 4)]
    part = to_all(part, "y", 8)
    mine = to_all(part, "x", 4)
    o, lse = attend_own(me, assignment, lengths, queries, own, interpret)
    mine, o, lse = lax.optimization_barrier((mine, o, lse))
    theirs = swap(mine, "core")
    out = attend_anchor(
        0, me, assignment, anchor, lengths, queries, mine, o, lse, None, interpret
    )
    return attend_anchor(
        1, me, assignment, anchor, lengths, queries, theirs, o, lse, out, interpret
    )


def shards(queries, keys, values, assignment, anchor, lengths):
    me = lax.axis_index(AXES).astype(jnp.int32).reshape(1)
    return run(me, queries, keys, values, assignment, anchor, lengths)


def solution(mesh):
    fine = Mesh(mesh.devices.reshape(SIZES), AXES)
    spec = P(AXES, None)
    return jax.shard_map(
        shards,
        mesh=fine,
        in_specs=(spec, spec, spec, P(), P(), P()),
        out_specs=spec,
        check_vma=False,
    )
```

```python
import functools
import math

import jax
import jax.numpy as jnp
from jax import lax
from jax.experimental import pallas as pl
from jax.experimental.pallas import tpu as pltpu
from jax.sharding import Mesh, PartitionSpec as P

HEAD_DIM = 128
GROUP = 8
KV_HEADS = 8
HALF = 4
WIDTH = GROUP * HEAD_DIM
AXES = ("y", "zl", "core", "x", "zh")
SIZES = (8, 4, 2, 4, 2)
CHUNK = 4
SCALE = math.log2(math.e) / math.sqrt(HEAD_DIM)
NEG = -math.inf


def group_columns(g):
    return pl.ds(pl.multiple_of(g * WIDTH, WIDTH), WIDTH)


def scores(q_ref, c, k):
    first = c * CHUNK * HEAD_DIM
    q = jnp.concatenate(
        [q_ref[:, first + i * HEAD_DIM : first + (i + 1) * HEAD_DIM] for i in range(CHUNK)], axis=0
    )
    return lax.dot_general(q, k, (((1,), (1,)), ((), ())), preferred_element_type=jnp.float32)


def softmax(s, bias):
    free = s.shape[1] - bias.shape[1]
    rows = s.shape[0] // CHUNK
    tail = (s[:, free:].reshape(CHUNK, rows, -1) + bias[None]).reshape(CHUNK * rows, -1)
    s = jnp.concatenate([s[:, :free], tail], axis=1) if free else tail
    m = jnp.max(s, axis=1, keepdims=True)
    e = jnp.exp2((s - m) * SCALE)
    return m, jnp.sum(e, axis=1, keepdims=True), e.astype(jnp.bfloat16)


def attend_heads(q_buf, heads, load, bias, finish):
    work = [(g, c) for g in heads for c in range(GROUP // CHUNK)]
    found, weighed, values = {}, {}, {}
    for t in range(len(work) + 2):
        if t < len(work):
            g, c = work[t]
            if c == 0:
                k, v = load(g)
            values[t] = v
            found[t] = scores(q_buf.at[g], c, k)
        if t >= 2:
            m, l, e = weighed.pop(t - 2)
            o = jnp.dot(e, values.pop(t - 2), preferred_element_type=jnp.float32)
            finish(*work[t - 2], m, l, o)
        if 1 <= t <= len(work):
            weighed[t - 1] = softmax(found.pop(t - 1), bias)


def query_copy(q_hbm, q_buf, sem, g):
    return pltpu.make_async_copy(q_hbm.at[:, group_columns(g)], q_buf.at[g], sem.at[g])


def start_ahead(copies, g, count=KV_HEADS):
    def start():
        for copy in copies(g):
            copy.start()

    if isinstance(g, int):
        if g < count:
            start()
    else:
        pl.when(g < count)(start)


def own_kernel(me, assignment, lengths, q_hbm, *refs):
    pairs_hbm, (o_hbm, lse_hbm) = refs[:4], refs[4:6]
    bias_ref, q_buf, kv_buf, o_buf, lse_buf, q_sem, kv_sem, o_sem, lse_sem = refs[6:]
    rows = q_buf.shape[1]

    def group_copies(g):
        return [query_copy(q_hbm, q_buf, q_sem, g)] + [
            pltpu.make_async_copy(ref.at[:, g & 3, :, g >> 2], kv_buf.at[g, i], kv_sem.at[i, g])
            for i, ref in enumerate(pairs_hbm)
        ]

    start_ahead(group_copies, 0)
    start_ahead(group_copies, 1)
    head_me = me[0] & 7
    my_len = lengths[assignment[me[0] >> 3]]
    col = lax.broadcasted_iota(jnp.int32, bias_ref.shape, 1)
    row = lax.broadcasted_iota(jnp.int32, bias_ref.shape, 0) + head_me * rows
    pos = (((head_me >> 1) - (col >> 7)) & 3) * 2 * rows + (col & 127)
    bias_ref[...] = jnp.where((pos <= row) & (pos < my_len), 0.0, NEG)
    def result_copies(g):
        return (
            pltpu.make_async_copy(o_buf.at[g], o_hbm.at[g], o_sem.at[g]),
            pltpu.make_async_copy(lse_buf.at[g], lse_hbm.at[g], lse_sem.at[g]),
        )

    def load(g):
        start_ahead(group_copies, g + 2)
        for copy in group_copies(g):
            copy.wait()
        return [kv_buf[g, :, :, kind].reshape(8 * rows, HEAD_DIM) for kind in range(2)]

    def finish(g, c, m, l, o):
        at = pl.ds(c * CHUNK * rows, CHUNK * rows)
        o_buf[g, at] = o * (1.0 / l)
        lse_buf[g, at] = jnp.broadcast_to(m * SCALE + jnp.log2(l), o.shape)
        if c == GROUP // CHUNK - 1:
            for copy in result_copies(g):
                copy.start()

    def step(i, carry):
        attend_heads(q_buf, [4 * i + j for j in range(4)], load, bias_ref[...], finish)
        return carry

    lax.fori_loop(0, KV_HEADS // 4, step, 0)
    for g in range(KV_HEADS):
        for copy in result_copies(g):
            copy.wait()


def anchor_kernel(which, me, assignment, anchor, lengths, q_hbm, kv_hbm, o_hbm, lse_hbm, *refs):
    out_hbm, bias_ref, q_buf, kv_buf, o_buf, lse_buf, out_buf, in_sem, out_sem = refs[-9:]
    rows = q_buf.shape[1]
    core = (me[0] >> 3) & 1
    first = (core ^ which) * HALF

    def group_copies(i):
        g = first + i
        return (
            pltpu.make_async_copy(q_hbm.at[:, group_columns(g)], q_buf.at[i], in_sem.at[0, i]),
            pltpu.make_async_copy(kv_hbm.at[:, pl.ds(2 * i, 2)], kv_buf.at[i], in_sem.at[1, i]),
            pltpu.make_async_copy(o_hbm.at[g], o_buf.at[i], in_sem.at[2, i]),
            pltpu.make_async_copy(lse_hbm.at[g], lse_buf.at[i], in_sem.at[3, i]),
        )

    def out_copy(i):
        to = out_hbm.at[:, group_columns(first + i)]
        return pltpu.make_async_copy(out_buf.at[i], to, out_sem.at[i])

    start_ahead(group_copies, 0)
    start_ahead(group_copies, 1)
    anc_len = lengths[anchor[0]]
    is_anchor = assignment[me[0] >> 3] == anchor[0]
    col = lax.broadcasted_iota(jnp.int32, bias_ref.shape, 1) + 256
    bias_ref[...] = jnp.where(col < anc_len, 0.0, NEG)

    def load(i):
        start_ahead(group_copies, i + 2, HALF)
        for copy in group_copies(i):
            copy.wait()
        return [kv_buf[i, :, kind].reshape(8 * rows, HEAD_DIM) for kind in range(2)]

    def finish(i, c, m1, l1, o1):
        at = pl.ds(c * CHUNK * rows, CHUNK * rows)
        lse1 = jnp.where(is_anchor, NEG, m1 * SCALE + jnp.log2(l1))
        share = 1.0 / (1.0 + jnp.exp2(lse_buf[i, at] - lse1))
        o = (1.0 - share) * o_buf[i, at] + (share * (1.0 / l1)) * o1
        o = o.astype(out_buf.dtype)
        for j in range(CHUNK):
            to = (c * CHUNK + j) * HEAD_DIM
            out_buf[i, :, to : to + HEAD_DIM] = o[j * rows : (j + 1) * rows]
        if c == GROUP // CHUNK - 1:
            out_copy(i).start()

    attend_heads(q_buf, list(range(HALF)), load, bias_ref[0:1, :], finish)
    for i in range(HALF):
        out_copy(i).wait()


VMEM = pl.BlockSpec(memory_space=pltpu.VMEM)
SMEM = pl.BlockSpec(memory_space=pltpu.SMEM)
ANY = pl.BlockSpec(memory_space=pl.ANY)
COST = pl.CostEstimate(flops=2**31, bytes_accessed=6 * 2**20, transcendentals=2**21)
LONG = pl.CostEstimate(flops=2**36, bytes_accessed=6 * 2**20, transcendentals=2**21)
PARAMS = pltpu.CompilerParams(vmem_limit_bytes=60 * 1024 * 1024)


def attend_own(me, assignment, lengths, queries, own, interpret=False):
    rows = queries.shape[0]
    part = jax.ShapeDtypeStruct((KV_HEADS, GROUP * rows, HEAD_DIM), jnp.float32)
    return pl.pallas_call(
        own_kernel,
        out_shape=(part, part),
        in_specs=[SMEM, SMEM, SMEM] + [ANY] * 5,
        out_specs=(ANY, ANY),
        scratch_shapes=[
            pltpu.VMEM((rows, 8 * rows), jnp.float32),
            pltpu.VMEM((KV_HEADS, rows, WIDTH), jnp.bfloat16),
            pltpu.VMEM((KV_HEADS, 4, 2, 2, rows, HEAD_DIM), jnp.bfloat16),
            pltpu.VMEM(part.shape, jnp.float32),
            pltpu.VMEM(part.shape, jnp.float32),
            pltpu.SemaphoreType.DMA((KV_HEADS,)),
            pltpu.SemaphoreType.DMA((4, KV_HEADS)),
            pltpu.SemaphoreType.DMA((KV_HEADS,)),
            pltpu.SemaphoreType.DMA((KV_HEADS,)),
        ],
        compiler_params=PARAMS,
        cost_estimate=LONG,
        interpret=interpret,
    )(me, assignment, lengths, queries, *own)


def attend_anchor(
    which, me, assignment, anchor, lengths, queries, kv, o, lse, out=None, interpret=False
):
    rows = queries.shape[0]
    extra = () if out is None else (out,)
    return pl.pallas_call(
        functools.partial(anchor_kernel, which),
        out_shape=jax.ShapeDtypeStruct(queries.shape, jnp.bfloat16),
        in_specs=[SMEM] * 4 + [ANY] * (4 + len(extra)),
        out_specs=ANY,
        input_output_aliases={8: 0} if extra else {},
        scratch_shapes=[
            pltpu.VMEM((8, 8 * rows - 256), jnp.float32),
            pltpu.VMEM((HALF, rows, WIDTH), jnp.bfloat16),
            pltpu.VMEM((HALF, 4, 2, 2, rows, HEAD_DIM), jnp.bfloat16),
            pltpu.VMEM((HALF,) + o.shape[1:], jnp.float32),
            pltpu.VMEM((HALF,) + o.shape[1:], jnp.float32),
            pltpu.VMEM((HALF, rows, WIDTH), jnp.bfloat16),
            pltpu.SemaphoreType.DMA((4, HALF)),
            pltpu.SemaphoreType.DMA((HALF,)),
        ],
        compiler_params=PARAMS,
        cost_estimate=COST,
        interpret=interpret,
    )(me, assignment, anchor, lengths, queries, kv, o, lse, *extra)


def pair_kernel(me, mine_ref, other_ref, pair_ref):
    zh = me[0] & 1
    pair_ref[zh] = mine_ref[...]
    pair_ref[1 - zh] = other_ref[...]


def make_pair(me, mine, other, interpret=False):
    return pl.pallas_call(
        pair_kernel,
        out_shape=jax.ShapeDtypeStruct((2,) + mine.shape, mine.dtype),
        in_specs=[SMEM, VMEM, VMEM],
        out_specs=VMEM,
        cost_estimate=LONG,
        interpret=interpret,
    )(me, mine, other)


def cut_kernel(k_ref, v_ref, piece_ref):
    for kind, ref in enumerate((k_ref, v_ref)):
        for g in range(KV_HEADS):
            piece_ref[g % HALF, kind, g // HALF] = ref[:, g * HEAD_DIM : (g + 1) * HEAD_DIM]


def cut(keys, values, interpret=False):
    return pl.pallas_call(
        cut_kernel,
        out_shape=jax.ShapeDtypeStruct((HALF, 2, 2, keys.shape[0], HEAD_DIM), keys.dtype),
        in_specs=[VMEM, VMEM],
        out_specs=VMEM,
        interpret=interpret,
    )(keys, values)


def to_all(a, axes, n):
    return exchange(jnp.broadcast_to(a[None], (n,) + a.shape), axes)


def swap(a, axis):
    return lax.ppermute(a, axis, [(0, 1), (1, 0)])


def exchange(a, axes):
    return lax.all_to_all(a, axes, split_axis=0, concat_axis=0, tiled=True)


def shift(a, axis, by):
    n = lax.axis_size(axis)
    return lax.ppermute(a, axis, [(i, (i + by) % n) for i in range(n)])


def run(me, queries, keys, values, assignment, anchor, lengths, interpret=False):
    ids = jnp.arange(assignment.shape[0], dtype=jnp.int32)
    anchor_shard = jnp.sum(jnp.where(assignment == anchor[0], ids, 0))
    pieces = cut(keys, values, interpret)
    got = exchange(pieces.reshape((16,) + pieces.shape[3:]), ("y", "core"))
    other = swap(pieces, "zh")
    source = (anchor_shard >> 3) * 2 + (anchor_shard & 1)
    part = lax.dynamic_index_in_dim(got, source, 0, keepdims=False)
    part = to_all(part, ("zl", "zh"), 8)
    part = part.reshape((4, 2) + part.shape[1:])
    part = lax.dynamic_index_in_dim(part, (anchor_shard >> 1) & 3, 0, keepdims=False)
    pair = make_pair(me, pieces, other, interpret)
    part, pair = lax.optimization_barrier((part, pair))
    own = [pair] + [shift(pair, "x", s) for s in range(1, 4)]
    part = to_all(part, "y", 8)
    mine = to_all(part, "x", 4)
    o, lse = attend_own(me, assignment, lengths, queries, own, interpret)
    mine, o, lse = lax.optimization_barrier((mine, o, lse))
    theirs = swap(mine, "core")
    out = attend_anchor(
        0, me, assignment, anchor, lengths, queries, mine, o, lse, None, interpret
    )
    return attend_anchor(
        1, me, assignment, anchor, lengths, queries, theirs, o, lse, out, interpret
    )


def shards(queries, keys, values, assignment, anchor, lengths):
    me = lax.axis_index(AXES).astype(jnp.int32).reshape(1)
    return run(me, queries, keys, values, assignment, anchor, lengths)


def solution(mesh):
    fine = Mesh(mesh.devices.reshape(SIZES), AXES)
    spec = P(AXES, None)
    return jax.shard_map(
        shards,
        mesh=fine,
        in_specs=(spec, spec, spec, P(), P(), P()),
        out_specs=spec,
        check_vma=False,
    )
```

```python
import functools
import math

import jax
import jax.numpy as jnp
from jax import lax
from jax.experimental import pallas as pl
from jax.experimental.pallas import tpu as pltpu
from jax.sharding import Mesh, PartitionSpec as P

HEAD_DIM = 128
GROUP = 8
KV_HEADS = 8
HALF = 4
WIDTH = GROUP * HEAD_DIM
AXES = ("y", "zl", "core", "x", "zh")
SIZES = (8, 4, 2, 4, 2)
CHUNK = 8
SCALE = math.log2(math.e) / math.sqrt(HEAD_DIM)
NEG = -math.inf


def group_columns(g):
    return pl.ds(pl.multiple_of(g * WIDTH, WIDTH), WIDTH)


def scores(q_ref, c, k):
    first = c * CHUNK * HEAD_DIM
    q = jnp.concatenate(
        [q_ref[:, first + i * HEAD_DIM : first + (i + 1) * HEAD_DIM] for i in range(CHUNK)], axis=0
    )
    return lax.dot_general(q, k, (((1,), (1,)), ((), ())), preferred_element_type=jnp.float32)


def softmax(s, bias):
    free = s.shape[1] - bias.shape[1]
    rows = s.shape[0] // CHUNK
    tail = (s[:, free:].reshape(CHUNK, rows, -1) + bias[None]).reshape(CHUNK * rows, -1)
    s = jnp.concatenate([s[:, :free], tail], axis=1) if free else tail
    m = jnp.max(s, axis=1, keepdims=True)
    e = jnp.exp2((s - m) * SCALE)
    return m, jnp.sum(e, axis=1, keepdims=True), e.astype(jnp.bfloat16)


def attend_heads(q_buf, heads, load, bias, finish):
    work = [(g, c) for g in heads for c in range(GROUP // CHUNK)]
    found, weighed, values = {}, {}, {}
    for t in range(len(work) + 2):
        if t < len(work):
            g, c = work[t]
            if c == 0:
                k, v = load(g)
            values[t] = v
            found[t] = scores(q_buf.at[g], c, k)
        if t >= 2:
            m, l, e = weighed.pop(t - 2)
            o = jnp.dot(e, values.pop(t - 2), preferred_element_type=jnp.float32)
            finish(*work[t - 2], m, l, o)
        if 1 <= t <= len(work):
            weighed[t - 1] = softmax(found.pop(t - 1), bias)


def query_copy(q_hbm, q_buf, sem, g):
    return pltpu.make_async_copy(q_hbm.at[:, group_columns(g)], q_buf.at[g], sem.at[g])


def start_ahead(copies, g, count=KV_HEADS):
    def start():
        for copy in copies(g):
            copy.start()

    if isinstance(g, int):
        if g < count:
            start()
    else:
        pl.when(g < count)(start)


def own_kernel(me, assignment, lengths, q_hbm, *refs):
    pairs_hbm, (o_hbm, lse_hbm) = refs[:4], refs[4:6]
    bias_ref, q_buf, kv_buf, o_buf, lse_buf, q_sem, kv_sem, o_sem, lse_sem = refs[6:]
    rows = q_buf.shape[1]

    def group_copies(g):
        return [query_copy(q_hbm, q_buf, q_sem, g)] + [
            pltpu.make_async_copy(ref.at[:, g & 3, :, g >> 2], kv_buf.at[g, i], kv_sem.at[i, g])
            for i, ref in enumerate(pairs_hbm)
        ]

    start_ahead(group_copies, 0)
    start_ahead(group_copies, 1)
    head_me = me[0] & 7
    my_len = lengths[assignment[me[0] >> 3]]
    col = lax.broadcasted_iota(jnp.int32, bias_ref.shape, 1)
    row = lax.broadcasted_iota(jnp.int32, bias_ref.shape, 0) + head_me * rows
    pos = (((head_me >> 1) - (col >> 7)) & 3) * 2 * rows + (col & 127)
    bias_ref[...] = jnp.where((pos <= row) & (pos < my_len), 0.0, NEG)
    def result_copies(g):
        return (
            pltpu.make_async_copy(o_buf.at[g], o_hbm.at[g], o_sem.at[g]),
            pltpu.make_async_copy(lse_buf.at[g], lse_hbm.at[g], lse_sem.at[g]),
        )

    def load(g):
        start_ahead(group_copies, g + 2)
        for copy in group_copies(g):
            copy.wait()
        return [kv_buf[g, :, :, kind].reshape(8 * rows, HEAD_DIM) for kind in range(2)]

    def finish(g, c, m, l, o):
        at = pl.ds(c * CHUNK * rows, CHUNK * rows)
        o_buf[g, at] = o * (1.0 / l)
        lse_buf[g, at] = jnp.broadcast_to(m * SCALE + jnp.log2(l), o.shape)
        if c == GROUP // CHUNK - 1:
            for copy in result_copies(g):
                copy.start()

    def step(i, carry):
        attend_heads(q_buf, [4 * i + j for j in range(4)], load, bias_ref[...], finish)
        return carry

    lax.fori_loop(0, KV_HEADS // 4, step, 0)
    for g in range(KV_HEADS):
        for copy in result_copies(g):
            copy.wait()


def anchor_kernel(which, me, assignment, anchor, lengths, q_hbm, kv_hbm, o_hbm, lse_hbm, *refs):
    out_hbm, bias_ref, q_buf, kv_buf, o_buf, lse_buf, out_buf, in_sem, out_sem = refs[-9:]
    rows = q_buf.shape[1]
    core = (me[0] >> 3) & 1
    first = (core ^ which) * HALF

    def group_copies(i):
        g = first + i
        return (
            pltpu.make_async_copy(q_hbm.at[:, group_columns(g)], q_buf.at[i], in_sem.at[0, i]),
            pltpu.make_async_copy(kv_hbm.at[:, pl.ds(2 * i, 2)], kv_buf.at[i], in_sem.at[1, i]),
            pltpu.make_async_copy(o_hbm.at[g], o_buf.at[i], in_sem.at[2, i]),
            pltpu.make_async_copy(lse_hbm.at[g], lse_buf.at[i], in_sem.at[3, i]),
        )

    def out_copy(i):
        to = out_hbm.at[:, group_columns(first + i)]
        return pltpu.make_async_copy(out_buf.at[i], to, out_sem.at[i])

    start_ahead(group_copies, 0)
    start_ahead(group_copies, 1)
    anc_len = lengths[anchor[0]]
    is_anchor = assignment[me[0] >> 3] == anchor[0]
    col = lax.broadcasted_iota(jnp.int32, bias_ref.shape, 1) + 256
    bias_ref[...] = jnp.where(col < anc_len, 0.0, NEG)

    def load(i):
        start_ahead(group_copies, i + 2, HALF)
        for copy in group_copies(i)[:2]:
            copy.wait()
        return [kv_buf[i, :, kind].reshape(8 * rows, HEAD_DIM) for kind in range(2)]

    def finish(i, c, m1, l1, o1):
        if c == 0:
            for copy in group_copies(i)[2:]:
                copy.wait()
        at = pl.ds(c * CHUNK * rows, CHUNK * rows)
        lse1 = jnp.where(is_anchor, NEG, m1 * SCALE + jnp.log2(l1))
        share = 1.0 / (1.0 + jnp.exp2(lse_buf[i, at] - lse1))
        o = (1.0 - share) * o_buf[i, at] + (share * (1.0 / l1)) * o1
        o = o.astype(out_buf.dtype)
        for j in range(CHUNK):
            to = (c * CHUNK + j) * HEAD_DIM
            out_buf[i, :, to : to + HEAD_DIM] = o[j * rows : (j + 1) * rows]
        if c == GROUP // CHUNK - 1:
            out_copy(i).start()

    attend_heads(q_buf, list(range(HALF)), load, bias_ref[0:1, :], finish)
    for i in range(HALF):
        out_copy(i).wait()


VMEM = pl.BlockSpec(memory_space=pltpu.VMEM)
SMEM = pl.BlockSpec(memory_space=pltpu.SMEM)
ANY = pl.BlockSpec(memory_space=pl.ANY)
COST = pl.CostEstimate(flops=2**31, bytes_accessed=6 * 2**20, transcendentals=2**21)
LONG = pl.CostEstimate(flops=2**36, bytes_accessed=6 * 2**20, transcendentals=2**21)
PARAMS = pltpu.CompilerParams(vmem_limit_bytes=60 * 1024 * 1024)


def attend_own(me, assignment, lengths, queries, own, interpret=False):
    rows = queries.shape[0]
    part = jax.ShapeDtypeStruct((KV_HEADS, GROUP * rows, HEAD_DIM), jnp.float32)
    return pl.pallas_call(
        own_kernel,
        out_shape=(part, part),
        in_specs=[SMEM, SMEM, SMEM] + [ANY] * 5,
        out_specs=(ANY, ANY),
        scratch_shapes=[
            pltpu.VMEM((rows, 8 * rows), jnp.float32),
            pltpu.VMEM((KV_HEADS, rows, WIDTH), jnp.bfloat16),
            pltpu.VMEM((KV_HEADS, 4, 2, 2, rows, HEAD_DIM), jnp.bfloat16),
            pltpu.VMEM(part.shape, jnp.float32),
            pltpu.VMEM(part.shape, jnp.float32),
            pltpu.SemaphoreType.DMA((KV_HEADS,)),
            pltpu.SemaphoreType.DMA((4, KV_HEADS)),
            pltpu.SemaphoreType.DMA((KV_HEADS,)),
            pltpu.SemaphoreType.DMA((KV_HEADS,)),
        ],
        compiler_params=PARAMS,
        cost_estimate=LONG,
        interpret=interpret,
    )(me, assignment, lengths, queries, *own)


def attend_anchor(
    which, me, assignment, anchor, lengths, queries, kv, o, lse, out=None, interpret=False
):
    rows = queries.shape[0]
    extra = () if out is None else (out,)
    return pl.pallas_call(
        functools.partial(anchor_kernel, which),
        out_shape=jax.ShapeDtypeStruct(queries.shape, jnp.bfloat16),
        in_specs=[SMEM] * 4 + [ANY] * (4 + len(extra)),
        out_specs=ANY,
        input_output_aliases={8: 0} if extra else {},
        scratch_shapes=[
            pltpu.VMEM((8, 8 * rows - 256), jnp.float32),
            pltpu.VMEM((HALF, rows, WIDTH), jnp.bfloat16),
            pltpu.VMEM((HALF, 4, 2, 2, rows, HEAD_DIM), jnp.bfloat16),
            pltpu.VMEM((HALF,) + o.shape[1:], jnp.float32),
            pltpu.VMEM((HALF,) + o.shape[1:], jnp.float32),
            pltpu.VMEM((HALF, rows, WIDTH), jnp.bfloat16),
            pltpu.SemaphoreType.DMA((4, HALF)),
            pltpu.SemaphoreType.DMA((HALF,)),
        ],
        compiler_params=PARAMS,
        cost_estimate=COST,
        interpret=interpret,
    )(me, assignment, anchor, lengths, queries, kv, o, lse, *extra)


def pair_kernel(me, mine_ref, other_ref, pair_ref):
    zh = me[0] & 1
    pair_ref[zh] = mine_ref[...]
    pair_ref[1 - zh] = other_ref[...]


def make_pair(me, mine, other, interpret=False):
    return pl.pallas_call(
        pair_kernel,
        out_shape=jax.ShapeDtypeStruct((2,) + mine.shape, mine.dtype),
        in_specs=[SMEM, VMEM, VMEM],
        out_specs=VMEM,
        cost_estimate=LONG,
        interpret=interpret,
    )(me, mine, other)


def cut_kernel(k_ref, v_ref, piece_ref):
    for kind, ref in enumerate((k_ref, v_ref)):
        for g in range(KV_HEADS):
            piece_ref[g % HALF, kind, g // HALF] = ref[:, g * HEAD_DIM : (g + 1) * HEAD_DIM]


def cut(keys, values, interpret=False):
    return pl.pallas_call(
        cut_kernel,
        out_shape=jax.ShapeDtypeStruct((HALF, 2, 2, keys.shape[0], HEAD_DIM), keys.dtype),
        in_specs=[VMEM, VMEM],
        out_specs=VMEM,
        interpret=interpret,
    )(keys, values)


def copies_kernel(a_ref, out_ref):
    for i in range(out_ref.shape[0]):
        out_ref[i] = a_ref[...]


def copies(a, n, interpret=False):
    return pl.pallas_call(
        copies_kernel,
        out_shape=jax.ShapeDtypeStruct((n,) + a.shape, a.dtype),
        in_specs=[VMEM],
        out_specs=VMEM,
        cost_estimate=LONG,
        interpret=interpret,
    )(a)


def to_all(a, axes, n):
    return exchange(jnp.broadcast_to(a[None], (n,) + a.shape), axes)


def swap(a, axis):
    return lax.ppermute(a, axis, [(0, 1), (1, 0)])


def exchange(a, axes):
    return lax.all_to_all(a, axes, split_axis=0, concat_axis=0, tiled=True)


def shift(a, axis, by):
    n = lax.axis_size(axis)
    return lax.ppermute(a, axis, [(i, (i + by) % n) for i in range(n)])


def run(me, queries, keys, values, assignment, anchor, lengths, interpret=False):
    ids = jnp.arange(assignment.shape[0], dtype=jnp.int32)
    anchor_shard = jnp.sum(jnp.where(assignment == anchor[0], ids, 0))
    pieces = cut(keys, values, interpret)
    got = exchange(pieces.reshape((16,) + pieces.shape[3:]), ("y", "core"))
    other = swap(pieces, "zh")
    source = (anchor_shard >> 3) * 2 + (anchor_shard & 1)
    part = lax.dynamic_index_in_dim(got, source, 0, keepdims=False)
    part = to_all(part, ("zl", "zh"), 8)
    part = part.reshape((4, 2) + part.shape[1:])
    part = lax.dynamic_index_in_dim(part, (anchor_shard >> 1) & 3, 0, keepdims=False)
    pair = make_pair(me, pieces, other, interpret)
    part, pair = lax.optimization_barrier((part, pair))
    ahead = shift(pair, "x", 3)
    own = [pair, shift(pair, "x", 1), shift(ahead, "x", 3), ahead]
    part = to_all(part, "y", 8)
    mine = exchange(copies(part, 4, interpret), "x")
    o, lse = attend_own(me, assignment, lengths, queries, own, interpret)
    mine, o, lse = lax.optimization_barrier((mine, o, lse))
    theirs = swap(mine, "core")
    out = attend_anchor(
        0, me, assignment, anchor, lengths, queries, mine, o, lse, None, interpret
    )
    return attend_anchor(
        1, me, assignment, anchor, lengths, queries, theirs, o, lse, out, interpret
    )


def shards(queries, keys, values, assignment, anchor, lengths):
    me = lax.axis_index(AXES).astype(jnp.int32).reshape(1)
    return run(me, queries, keys, values, assignment, anchor, lengths)


def solution(mesh):
    fine = Mesh(mesh.devices.reshape(SIZES), AXES)
    spec = P(AXES, None)
    return jax.shard_map(
        shards,
        mesh=fine,
        in_specs=(spec, spec, spec, P(), P(), P()),
        out_specs=spec,
        check_vma=False,
    )
```

```python
import functools
import math

import jax
import jax.numpy as jnp
from jax import lax
from jax.experimental import pallas as pl
from jax.experimental.pallas import tpu as pltpu
from jax.sharding import Mesh, PartitionSpec as P

HEAD_DIM = 128
GROUP = 8
KV_HEADS = 8
HALF = 4
WIDTH = GROUP * HEAD_DIM
AXES = ("y", "zl", "core", "x", "zh")
SIZES = (8, 4, 2, 4, 2)
OWN_CHUNK = 4
ANCHOR_CHUNK = 2
SCALE = math.log2(math.e) / math.sqrt(HEAD_DIM)
NEG = -math.inf


def group_columns(g):
    return pl.ds(pl.multiple_of(g * WIDTH, WIDTH), WIDTH)


def scores(q_ref, c, chunk, k):
    first = c * chunk * HEAD_DIM
    q = jnp.concatenate(
        [q_ref[:, first + i * HEAD_DIM : first + (i + 1) * HEAD_DIM] for i in range(chunk)], axis=0
    )
    return lax.dot_general(q, k, (((1,), (1,)), ((), ())), preferred_element_type=jnp.float32)


def softmax(s, chunk, bias):
    free = s.shape[1] - bias.shape[1]
    rows = s.shape[0] // chunk
    tail = (s[:, free:].reshape(chunk, rows, -1) + bias[None]).reshape(chunk * rows, -1)
    s = jnp.concatenate([s[:, :free], tail], axis=1) if free else tail
    m = jnp.max(s, axis=1, keepdims=True)
    e = jnp.exp2((s - m) * SCALE)
    return m, jnp.sum(e, axis=1, keepdims=True), e.astype(jnp.bfloat16)


def attend_heads(q_buf, heads, chunk, load, bias, finish):
    work = [(g, c) for g in heads for c in range(GROUP // chunk)]
    found, weighed, values = {}, {}, {}
    for t in range(len(work) + 2):
        if t < len(work):
            g, c = work[t]
            if c == 0:
                k, v = load(g)
            values[t] = v
            found[t] = scores(q_buf.at[g], c, chunk, k)
        if t >= 2:
            m, l, e = weighed.pop(t - 2)
            o = jnp.dot(e, values.pop(t - 2), preferred_element_type=jnp.float32)
            finish(*work[t - 2], m, l, o)
        if 1 <= t <= len(work):
            weighed[t - 1] = softmax(found.pop(t - 1), chunk, bias)


def query_copy(q_hbm, q_buf, sem, g):
    return pltpu.make_async_copy(q_hbm.at[:, group_columns(g)], q_buf.at[g], sem.at[g])


def start_ahead(copies, g, count=KV_HEADS):
    def start():
        for copy in copies(g):
            copy.start()

    if isinstance(g, int):
        if g < count:
            start()
    else:
        pl.when(g < count)(start)


def own_kernel(me, assignment, lengths, q_hbm, *refs):
    pairs_hbm, (o_hbm, lse_hbm) = refs[:4], refs[4:6]
    bias_ref, q_buf, kv_buf, o_buf, lse_buf, q_sem, kv_sem, o_sem, lse_sem = refs[6:]
    rows = q_buf.shape[1]

    def group_copies(g):
        return [query_copy(q_hbm, q_buf, q_sem, g)] + [
            pltpu.make_async_copy(ref.at[:, g & 3, :, g >> 2], kv_buf.at[g, i], kv_sem.at[i, g])
            for i, ref in enumerate(pairs_hbm)
        ]

    start_ahead(group_copies, 0)
    start_ahead(group_copies, 1)
    head_me = me[0] & 7
    my_len = lengths[assignment[me[0] >> 3]]
    col = lax.broadcasted_iota(jnp.int32, bias_ref.shape, 1)
    row = lax.broadcasted_iota(jnp.int32, bias_ref.shape, 0) + head_me * rows
    pos = (((head_me >> 1) - (col >> 7)) & 3) * 2 * rows + (col & 127)
    bias_ref[...] = jnp.where((pos <= row) & (pos < my_len), 0.0, NEG)
    def result_copies(g):
        return (
            pltpu.make_async_copy(o_buf.at[g], o_hbm.at[g], o_sem.at[g]),
            pltpu.make_async_copy(lse_buf.at[g], lse_hbm.at[g], lse_sem.at[g]),
        )

    def load(g):
        start_ahead(group_copies, g + 2)
        for copy in group_copies(g):
            copy.wait()
        return [kv_buf[g, :, :, kind].reshape(8 * rows, HEAD_DIM) for kind in range(2)]

    def finish(g, c, m, l, o):
        at = pl.ds(c * OWN_CHUNK * rows, OWN_CHUNK * rows)
        o_buf[g, at] = o * (1.0 / l)
        lse_buf[g, at] = jnp.broadcast_to(m * SCALE + jnp.log2(l), o.shape)
        if c == GROUP // OWN_CHUNK - 1:
            for copy in result_copies(g):
                copy.start()

    def step(i, carry):
        attend_heads(q_buf, [4 * i + j for j in range(4)], OWN_CHUNK, load, bias_ref[...], finish)
        return carry

    lax.fori_loop(0, KV_HEADS // 4, step, 0)
    for g in range(KV_HEADS):
        for copy in result_copies(g):
            copy.wait()


def anchor_kernel(which, me, assignment, anchor, lengths, q_hbm, kv_hbm, o_hbm, lse_hbm, *refs):
    out_hbm, bias_ref, q_buf, kv_buf, o_buf, lse_buf, out_buf, in_sem, out_sem = refs[-9:]
    rows = q_buf.shape[1]
    core = (me[0] >> 3) & 1
    first = (core ^ which) * HALF

    def group_copies(i):
        g = first + i
        return (
            pltpu.make_async_copy(q_hbm.at[:, group_columns(g)], q_buf.at[i], in_sem.at[0, i]),
            pltpu.make_async_copy(kv_hbm.at[:, pl.ds(2 * i, 2)], kv_buf.at[i], in_sem.at[1, i]),
            pltpu.make_async_copy(o_hbm.at[g], o_buf.at[i], in_sem.at[2, i]),
            pltpu.make_async_copy(lse_hbm.at[g], lse_buf.at[i], in_sem.at[3, i]),
        )

    def out_copy(i):
        to = out_hbm.at[:, group_columns(first + i)]
        return pltpu.make_async_copy(out_buf.at[i], to, out_sem.at[i])

    start_ahead(group_copies, 0)
    start_ahead(group_copies, 1)
    anc_len = lengths[anchor[0]]
    is_anchor = assignment[me[0] >> 3] == anchor[0]
    col = lax.broadcasted_iota(jnp.int32, bias_ref.shape, 1) + 256
    bias_ref[...] = jnp.where(col < anc_len, 0.0, NEG)

    def load(i):
        start_ahead(group_copies, i + 2, HALF)
        for copy in group_copies(i):
            copy.wait()
        return [kv_buf[i, :, kind].reshape(8 * rows, HEAD_DIM) for kind in range(2)]

    def finish(i, c, m1, l1, o1):
        at = pl.ds(c * ANCHOR_CHUNK * rows, ANCHOR_CHUNK * rows)
        lse1 = jnp.where(is_anchor, NEG, m1 * SCALE + jnp.log2(l1))
        share = 1.0 / (1.0 + jnp.exp2(lse_buf[i, at] - lse1))
        o = (1.0 - share) * o_buf[i, at] + (share * (1.0 / l1)) * o1
        o = o.astype(out_buf.dtype)
        for j in range(ANCHOR_CHUNK):
            to = (c * ANCHOR_CHUNK + j) * HEAD_DIM
            out_buf[i, :, to : to + HEAD_DIM] = o[j * rows : (j + 1) * rows]
        if c == GROUP // ANCHOR_CHUNK - 1:
            out_copy(i).start()

    attend_heads(q_buf, list(range(HALF)), ANCHOR_CHUNK, load, bias_ref[0:1, :], finish)
    for i in range(HALF):
        out_copy(i).wait()


VMEM = pl.BlockSpec(memory_space=pltpu.VMEM)
SMEM = pl.BlockSpec(memory_space=pltpu.SMEM)
ANY = pl.BlockSpec(memory_space=pl.ANY)
COST = pl.CostEstimate(flops=2**31, bytes_accessed=6 * 2**20, transcendentals=2**21)
LONG = pl.CostEstimate(flops=2**36, bytes_accessed=6 * 2**20, transcendentals=2**21)
PARAMS = pltpu.CompilerParams(vmem_limit_bytes=60 * 1024 * 1024)


def attend_own(me, assignment, lengths, queries, own, interpret=False):
    rows = queries.shape[0]
    part = jax.ShapeDtypeStruct((KV_HEADS, GROUP * rows, HEAD_DIM), jnp.float32)
    return pl.pallas_call(
        own_kernel,
        out_shape=(part, part),
        in_specs=[SMEM, SMEM, SMEM] + [ANY] * 5,
        out_specs=(ANY, ANY),
        scratch_shapes=[
            pltpu.VMEM((rows, 8 * rows), jnp.float32),
            pltpu.VMEM((KV_HEADS, rows, WIDTH), jnp.bfloat16),
            pltpu.VMEM((KV_HEADS, 4, 2, 2, rows, HEAD_DIM), jnp.bfloat16),
            pltpu.VMEM(part.shape, jnp.float32),
            pltpu.VMEM(part.shape, jnp.float32),
            pltpu.SemaphoreType.DMA((KV_HEADS,)),
            pltpu.SemaphoreType.DMA((4, KV_HEADS)),
            pltpu.SemaphoreType.DMA((KV_HEADS,)),
            pltpu.SemaphoreType.DMA((KV_HEADS,)),
        ],
        compiler_params=PARAMS,
        cost_estimate=LONG,
        interpret=interpret,
    )(me, assignment, lengths, queries, *own)


def attend_anchor(
    which, me, assignment, anchor, lengths, queries, kv, o, lse, out=None, interpret=False
):
    rows = queries.shape[0]
    extra = () if out is None else (out,)
    return pl.pallas_call(
        functools.partial(anchor_kernel, which),
        out_shape=jax.ShapeDtypeStruct(queries.shape, jnp.bfloat16),
        in_specs=[SMEM] * 4 + [ANY] * (4 + len(extra)),
        out_specs=ANY,
        input_output_aliases={8: 0} if extra else {},
        scratch_shapes=[
            pltpu.VMEM((8, 8 * rows - 256), jnp.float32),
            pltpu.VMEM((HALF, rows, WIDTH), jnp.bfloat16),
            pltpu.VMEM((HALF, 4, 2, 2, rows, HEAD_DIM), jnp.bfloat16),
            pltpu.VMEM((HALF,) + o.shape[1:], jnp.float32),
            pltpu.VMEM((HALF,) + o.shape[1:], jnp.float32),
            pltpu.VMEM((HALF, rows, WIDTH), jnp.bfloat16),
            pltpu.SemaphoreType.DMA((4, HALF)),
            pltpu.SemaphoreType.DMA((HALF,)),
        ],
        compiler_params=PARAMS,
        cost_estimate=COST,
        interpret=interpret,
    )(me, assignment, anchor, lengths, queries, kv, o, lse, *extra)


def pair_kernel(me, mine_ref, other_ref, pair_ref):
    zh = me[0] & 1
    pair_ref[zh] = mine_ref[...]
    pair_ref[1 - zh] = other_ref[...]


def make_pair(me, mine, other, interpret=False):
    return pl.pallas_call(
        pair_kernel,
        out_shape=jax.ShapeDtypeStruct((2,) + mine.shape, mine.dtype),
        in_specs=[SMEM, VMEM, VMEM],
        out_specs=VMEM,
        cost_estimate=LONG,
        interpret=interpret,
    )(me, mine, other)


def cut_kernel(k_ref, v_ref, piece_ref):
    for kind, ref in enumerate((k_ref, v_ref)):
        for g in range(KV_HEADS):
            piece_ref[g % HALF, kind, g // HALF] = ref[:, g * HEAD_DIM : (g + 1) * HEAD_DIM]


def cut(keys, values, interpret=False):
    return pl.pallas_call(
        cut_kernel,
        out_shape=jax.ShapeDtypeStruct((HALF, 2, 2, keys.shape[0], HEAD_DIM), keys.dtype),
        in_specs=[VMEM, VMEM],
        out_specs=VMEM,
        interpret=interpret,
    )(keys, values)


def hold(a, interpret=False):
    return pl.pallas_call(
        lambda a_ref, out_ref: None,
        out_shape=jax.ShapeDtypeStruct(a.shape, a.dtype),
        in_specs=[ANY],
        out_specs=ANY,
        input_output_aliases={0: 0},
        cost_estimate=LONG,
        interpret=interpret,
    )(a)


def to_all(a, axes, n):
    return exchange(jnp.broadcast_to(a[None], (n,) + a.shape), axes)


def swap(a, axis):
    return lax.ppermute(a, axis, [(0, 1), (1, 0)])


def exchange(a, axes):
    return lax.all_to_all(a, axes, split_axis=0, concat_axis=0, tiled=True)


def shift(a, axis, by):
    n = lax.axis_size(axis)
    return lax.ppermute(a, axis, [(i, (i + by) % n) for i in range(n)])


def run(me, queries, keys, values, assignment, anchor, lengths, interpret=False):
    ids = jnp.arange(assignment.shape[0], dtype=jnp.int32)
    anchor_shard = jnp.sum(jnp.where(assignment == anchor[0], ids, 0))
    pieces = cut(keys, values, interpret)
    got = exchange(pieces.reshape((16,) + pieces.shape[3:]), ("y", "core"))
    other = swap(pieces, "zh")
    source = (anchor_shard >> 3) * 2 + (anchor_shard & 1)
    part = lax.dynamic_index_in_dim(got, source, 0, keepdims=False)
    part = to_all(part, ("zl", "zh"), 8)
    part = part.reshape((4, 2) + part.shape[1:])
    part = lax.dynamic_index_in_dim(part, (anchor_shard >> 1) & 3, 0, keepdims=False)
    pair = make_pair(me, pieces, other, interpret)
    part, pair = lax.optimization_barrier((part, pair))
    ahead = shift(pair, "x", 3)
    own = [pair, shift(pair, "x", 1), shift(ahead, "x", 3), ahead]
    part = to_all(part, "y", 8)
    mine = to_all(hold(part, interpret), "x", 4)
    o, lse = attend_own(me, assignment, lengths, queries, own, interpret)
    mine, o, lse = lax.optimization_barrier((mine, o, lse))
    theirs = swap(mine, "core")
    out = attend_anchor(
        0, me, assignment, anchor, lengths, queries, mine, o, lse, None, interpret
    )
    return attend_anchor(
        1, me, assignment, anchor, lengths, queries, theirs, o, lse, out, interpret
    )


def shards(queries, keys, values, assignment, anchor, lengths):
    me = lax.axis_index(AXES).astype(jnp.int32).reshape(1)
    return run(me, queries, keys, values, assignment, anchor, lengths)


def solution(mesh):
    fine = Mesh(mesh.devices.reshape(SIZES), AXES)
    spec = P(AXES, None)
    return jax.shard_map(
        shards,
        mesh=fine,
        in_specs=(spec, spec, spec, P(), P(), P()),
        out_specs=spec,
        check_vma=False,
    )
```

```python
import functools
import math

import jax
import jax.numpy as jnp
from jax import lax
from jax.experimental import pallas as pl
from jax.experimental.pallas import tpu as pltpu
from jax.sharding import Mesh, PartitionSpec as P

HEAD_DIM = 128
GROUP = 8
KV_HEADS = 8
HALF = 4
WIDTH = GROUP * HEAD_DIM
AXES = ("y", "zl", "core", "x", "zh")
SIZES = (8, 4, 2, 4, 2)
OWN_CHUNK = 4
ANCHOR_CHUNK = 4
SCALE = math.log2(math.e) / math.sqrt(HEAD_DIM)
NEG = -math.inf


def group_columns(g):
    return pl.ds(pl.multiple_of(g * WIDTH, WIDTH), WIDTH)


def scores(q_ref, c, chunk, k):
    first = c * chunk * HEAD_DIM
    q = jnp.concatenate(
        [q_ref[:, first + i * HEAD_DIM : first + (i + 1) * HEAD_DIM] for i in range(chunk)], axis=0
    )
    return lax.dot_general(q, k, (((1,), (1,)), ((), ())), preferred_element_type=jnp.float32)


def softmax(s, chunk, bias):
    free = s.shape[1] - bias.shape[1]
    rows = s.shape[0] // chunk
    tail = (s[:, free:].reshape(chunk, rows, -1) + bias[None]).reshape(chunk * rows, -1)
    s = jnp.concatenate([s[:, :free], tail], axis=1) if free else tail
    m = jnp.max(s, axis=1, keepdims=True)
    e = jnp.exp2((s - m) * SCALE)
    return m, jnp.sum(e, axis=1, keepdims=True), e.astype(jnp.bfloat16)


def attend_heads(q_buf, heads, chunk, load, bias, finish):
    work = [(g, c) for g in heads for c in range(GROUP // chunk)]
    found, weighed, values = {}, {}, {}
    for t in range(len(work) + 2):
        if t < len(work):
            g, c = work[t]
            if c == 0:
                k, v = load(g)
            values[t] = v
            found[t] = scores(q_buf.at[g], c, chunk, k)
        if t >= 2:
            m, l, e = weighed.pop(t - 2)
            o = jnp.dot(e, values.pop(t - 2), preferred_element_type=jnp.float32)
            finish(*work[t - 2], m, l, o)
        if 1 <= t <= len(work):
            weighed[t - 1] = softmax(found.pop(t - 1), chunk, bias)


def query_copy(q_hbm, q_buf, sem, g):
    return pltpu.make_async_copy(q_hbm.at[:, group_columns(g)], q_buf.at[g], sem.at[g])


def start_ahead(copies, g, count=KV_HEADS):
    def start():
        for copy in copies(g):
            copy.start()

    if isinstance(g, int):
        if g < count:
            start()
    else:
        pl.when(g < count)(start)


def own_kernel(me, assignment, lengths, q_hbm, *refs):
    pairs_hbm, (o_hbm, lse_hbm) = refs[:4], refs[4:6]
    bias_ref, q_buf, kv_buf, o_buf, lse_buf, q_sem, kv_sem, o_sem, lse_sem = refs[6:]
    rows = q_buf.shape[1]

    def group_copies(g):
        return [query_copy(q_hbm, q_buf, q_sem, g)] + [
            pltpu.make_async_copy(ref.at[:, g & 3, :, g >> 2], kv_buf.at[g, i], kv_sem.at[i, g])
            for i, ref in enumerate(pairs_hbm)
        ]

    start_ahead(group_copies, 0)
    start_ahead(group_copies, 1)
    head_me = me[0] & 7
    my_len = lengths[assignment[me[0] >> 3]]
    col = lax.broadcasted_iota(jnp.int32, bias_ref.shape, 1)
    row = lax.broadcasted_iota(jnp.int32, bias_ref.shape, 0) + head_me * rows
    pos = (((head_me >> 1) - (col >> 7)) & 3) * 2 * rows + (col & 127)
    bias_ref[...] = jnp.where((pos <= row) & (pos < my_len), 0.0, NEG)
    def result_copies(g):
        return (
            pltpu.make_async_copy(o_buf.at[g], o_hbm.at[g], o_sem.at[g]),
            pltpu.make_async_copy(lse_buf.at[g], lse_hbm.at[g], lse_sem.at[g]),
        )

    def load(g):
        start_ahead(group_copies, g + 2)
        for copy in group_copies(g):
            copy.wait()
        return [kv_buf[g, :, :, kind].reshape(8 * rows, HEAD_DIM) for kind in range(2)]

    def finish(g, c, m, l, o):
        at = pl.ds(c * OWN_CHUNK * rows, OWN_CHUNK * rows)
        o_buf[g, at] = o * (1.0 / l)
        lse_buf[g, at] = jnp.broadcast_to(m * SCALE + jnp.log2(l), o.shape)
        if c == GROUP // OWN_CHUNK - 1:
            for copy in result_copies(g):
                copy.start()

    def step(i, carry):
        attend_heads(q_buf, [4 * i + j for j in range(4)], OWN_CHUNK, load, bias_ref[...], finish)
        return carry

    lax.fori_loop(0, KV_HEADS // 4, step, 0)
    for g in range(KV_HEADS):
        for copy in result_copies(g):
            copy.wait()


def anchor_kernel(which, me, assignment, anchor, lengths, q_hbm, kv_hbm, o_hbm, lse_hbm, *refs):
    out_hbm, bias_ref, q_buf, kv_buf, o_buf, lse_buf, out_buf, in_sem, out_sem = refs[-9:]
    rows = q_buf.shape[1]
    core = (me[0] >> 3) & 1
    first = (core ^ which) * HALF

    def group_copies(i):
        g = first + i
        return (
            pltpu.make_async_copy(q_hbm.at[:, group_columns(g)], q_buf.at[i], in_sem.at[0, i]),
            pltpu.make_async_copy(kv_hbm.at[:, pl.ds(2 * i, 2)], kv_buf.at[i], in_sem.at[1, i]),
            pltpu.make_async_copy(o_hbm.at[g], o_buf.at[i], in_sem.at[2, i]),
            pltpu.make_async_copy(lse_hbm.at[g], lse_buf.at[i], in_sem.at[3, i]),
        )

    def out_copy(i):
        to = out_hbm.at[:, group_columns(first + i)]
        return pltpu.make_async_copy(out_buf.at[i], to, out_sem.at[i])

    start_ahead(group_copies, 0)
    start_ahead(group_copies, 1)
    anc_len = lengths[anchor[0]]
    is_anchor = assignment[me[0] >> 3] == anchor[0]
    col = lax.broadcasted_iota(jnp.int32, bias_ref.shape, 1) + 256
    bias_ref[...] = jnp.where(col < anc_len, 0.0, NEG)

    def load(i):
        start_ahead(group_copies, i + 2, HALF)
        for copy in group_copies(i):
            copy.wait()
        return [kv_buf[i, :, kind].reshape(8 * rows, HEAD_DIM) for kind in range(2)]

    def finish(i, c, m1, l1, o1):
        at = pl.ds(c * ANCHOR_CHUNK * rows, ANCHOR_CHUNK * rows)
        lse1 = jnp.where(is_anchor, NEG, m1 * SCALE + jnp.log2(l1))
        share = 1.0 / (1.0 + jnp.exp2(lse_buf[i, at] - lse1))
        o = (1.0 - share) * o_buf[i, at] + (share * (1.0 / l1)) * o1
        o = o.astype(out_buf.dtype)
        for j in range(ANCHOR_CHUNK):
            to = (c * ANCHOR_CHUNK + j) * HEAD_DIM
            out_buf[i, :, to : to + HEAD_DIM] = o[j * rows : (j + 1) * rows]
        if c == GROUP // ANCHOR_CHUNK - 1:
            out_copy(i).start()

    attend_heads(q_buf, list(range(HALF)), ANCHOR_CHUNK, load, bias_ref[0:1, :], finish)
    for i in range(HALF):
        out_copy(i).wait()


VMEM = pl.BlockSpec(memory_space=pltpu.VMEM)
SMEM = pl.BlockSpec(memory_space=pltpu.SMEM)
ANY = pl.BlockSpec(memory_space=pl.ANY)
COST = pl.CostEstimate(flops=2**31, bytes_accessed=6 * 2**20, transcendentals=2**21)
LONG = pl.CostEstimate(flops=2**36, bytes_accessed=6 * 2**20, transcendentals=2**21)
PARAMS = pltpu.CompilerParams(vmem_limit_bytes=60 * 1024 * 1024)


def attend_own(me, assignment, lengths, queries, own, interpret=False):
    rows = queries.shape[0]
    part = jax.ShapeDtypeStruct((KV_HEADS, GROUP * rows, HEAD_DIM), jnp.float32)
    return pl.pallas_call(
        own_kernel,
        out_shape=(part, part),
        in_specs=[SMEM, SMEM, SMEM] + [ANY] * 5,
        out_specs=(ANY, ANY),
        scratch_shapes=[
            pltpu.VMEM((rows, 8 * rows), jnp.float32),
            pltpu.VMEM((KV_HEADS, rows, WIDTH), jnp.bfloat16),
            pltpu.VMEM((KV_HEADS, 4, 2, 2, rows, HEAD_DIM), jnp.bfloat16),
            pltpu.VMEM(part.shape, jnp.float32),
            pltpu.VMEM(part.shape, jnp.float32),
            pltpu.SemaphoreType.DMA((KV_HEADS,)),
            pltpu.SemaphoreType.DMA((4, KV_HEADS)),
            pltpu.SemaphoreType.DMA((KV_HEADS,)),
            pltpu.SemaphoreType.DMA((KV_HEADS,)),
        ],
        compiler_params=PARAMS,
        cost_estimate=LONG,
        interpret=interpret,
    )(me, assignment, lengths, queries, *own)


def attend_anchor(
    which, me, assignment, anchor, lengths, queries, kv, o, lse, out=None, interpret=False
):
    rows = queries.shape[0]
    extra = () if out is None else (out,)
    return pl.pallas_call(
        functools.partial(anchor_kernel, which),
        out_shape=jax.ShapeDtypeStruct(queries.shape, jnp.bfloat16),
        in_specs=[SMEM] * 4 + [ANY] * (4 + len(extra)),
        out_specs=ANY,
        input_output_aliases={8: 0} if extra else {},
        scratch_shapes=[
            pltpu.VMEM((8, 8 * rows - 256), jnp.float32),
            pltpu.VMEM((HALF, rows, WIDTH), jnp.bfloat16),
            pltpu.VMEM((HALF, 4, 2, 2, rows, HEAD_DIM), jnp.bfloat16),
            pltpu.VMEM((HALF,) + o.shape[1:], jnp.float32),
            pltpu.VMEM((HALF,) + o.shape[1:], jnp.float32),
            pltpu.VMEM((HALF, rows, WIDTH), jnp.bfloat16),
            pltpu.SemaphoreType.DMA((4, HALF)),
            pltpu.SemaphoreType.DMA((HALF,)),
        ],
        compiler_params=PARAMS,
        cost_estimate=COST,
        interpret=interpret,
    )(me, assignment, anchor, lengths, queries, kv, o, lse, *extra)


def pair_kernel(me, mine_ref, other_ref, pair_ref):
    zh = me[0] & 1
    pair_ref[zh] = mine_ref[...]
    pair_ref[1 - zh] = other_ref[...]


def make_pair(me, mine, other, interpret=False):
    return pl.pallas_call(
        pair_kernel,
        out_shape=jax.ShapeDtypeStruct((2,) + mine.shape, mine.dtype),
        in_specs=[SMEM, VMEM, VMEM],
        out_specs=VMEM,
        cost_estimate=LONG,
        interpret=interpret,
    )(me, mine, other)


def cut_kernel(k_ref, v_ref, piece_ref):
    for kind, ref in enumerate((k_ref, v_ref)):
        for g in range(KV_HEADS):
            piece_ref[g % HALF, kind, g // HALF] = ref[:, g * HEAD_DIM : (g + 1) * HEAD_DIM]


def cut(keys, values, interpret=False):
    return pl.pallas_call(
        cut_kernel,
        out_shape=jax.ShapeDtypeStruct((HALF, 2, 2, keys.shape[0], HEAD_DIM), keys.dtype),
        in_specs=[VMEM, VMEM],
        out_specs=VMEM,
        interpret=interpret,
    )(keys, values)


def hold_kernel(a_ref, out_ref):
    out_ref[...] = a_ref[...]


def hold(a, interpret=False):
    return pl.pallas_call(
        hold_kernel,
        out_shape=jax.ShapeDtypeStruct(a.shape, a.dtype),
        in_specs=[VMEM],
        out_specs=VMEM,
        cost_estimate=LONG,
        interpret=interpret,
    )(a)


def to_all(a, axes, n):
    return exchange(jnp.broadcast_to(a[None], (n,) + a.shape), axes)


def swap(a, axis):
    return lax.ppermute(a, axis, [(0, 1), (1, 0)])


def exchange(a, axes):
    return lax.all_to_all(a, axes, split_axis=0, concat_axis=0, tiled=True)


def shift(a, axis, by):
    n = lax.axis_size(axis)
    return lax.ppermute(a, axis, [(i, (i + by) % n) for i in range(n)])


def run(me, queries, keys, values, assignment, anchor, lengths, interpret=False):
    ids = jnp.arange(assignment.shape[0], dtype=jnp.int32)
    anchor_shard = jnp.sum(jnp.where(assignment == anchor[0], ids, 0))
    pieces = cut(keys, values, interpret)
    got = exchange(pieces.reshape((16,) + pieces.shape[3:]), ("y", "core"))
    other = swap(pieces, "zh")
    source = (anchor_shard >> 3) * 2 + (anchor_shard & 1)
    part = lax.dynamic_index_in_dim(got, source, 0, keepdims=False)
    part = to_all(part, ("zl", "zh"), 8)
    part = part.reshape((4, 2) + part.shape[1:])
    part = lax.dynamic_index_in_dim(part, (anchor_shard >> 1) & 3, 0, keepdims=False)
    pair = make_pair(me, pieces, other, interpret)
    part, pair = lax.optimization_barrier((part, pair))
    ahead = shift(pair, "x", 3)
    own = [pair, shift(pair, "x", 1), shift(ahead, "x", 3), ahead]
    part = to_all(part, "y", 8)
    mine = to_all(hold(part, interpret), "x", 4)
    o, lse = attend_own(me, assignment, lengths, queries, own, interpret)
    mine, o, lse = lax.optimization_barrier((mine, o, lse))
    theirs = swap(mine, "core")
    out = attend_anchor(
        0, me, assignment, anchor, lengths, queries, mine, o, lse, None, interpret
    )
    return attend_anchor(
        1, me, assignment, anchor, lengths, queries, theirs, o, lse, out, interpret
    )


def shards(queries, keys, values, assignment, anchor, lengths):
    me = lax.axis_index(AXES).astype(jnp.int32).reshape(1)
    return run(me, queries, keys, values, assignment, anchor, lengths)


def solution(mesh):
    fine = Mesh(mesh.devices.reshape(SIZES), AXES)
    spec = P(AXES, None)
    return jax.shard_map(
        shards,
        mesh=fine,
        in_specs=(spec, spec, spec, P(), P(), P()),
        out_specs=spec,
        check_vma=False,
    )
```
